32 devices in a mesh: band: 8 (over y, x, core), head: 4 (over z).
Axes of the slice: x: 2, y: 2, z: 4, core: 2. Of those that a mesh axis runs over, the one named last changes fastest.
Arguments:
- queries: bfloat16 [1024, 1536], P('band', 'head'), as said below
- keys: bfloat16 [1024, 1536], P('band', 'head'), as said below
- values: bfloat16 [1024, 1536], P('band', 'head'), may hold values from -6 to 6
- d_out: bfloat16 [1024, 1536], P('band', 'head'), may hold values from -6 to 6
- gain: float32 [1536], P('head'), may hold values from 0.1 to 1.9
- blocks_on: int32 [8, 4], P('band'), may hold values 0 or 1
Outputs:
- out: bfloat16 [1024, 1536], P('band', 'head')
- d_queries: bfloat16 [1024, 1536], P('band', 'head')
- d_keys: bfloat16 [1024, 1536], P('band', 'head')
- d_values: bfloat16 [1024, 1536], P('band', 'head')
The draws below stay inside these ranges and needn't reach their ends.
Inputs may be any that keep to these rules, and one draw needn't show every extreme that they name: `queries`: entries lie within -180 to 180. `keys`: entries lie within -6 to 6.
All inputs are finite; a program needn't handle non-finite values. No bound on the sum of `blocks_on` on one device may be relied on, other than what follows from the above.
Results may differ from the reference program's by a relative error of at most 0.0063.
Values may be sent and summed in bfloat16 or wider, within the bound.
No kernel may reach another device: no remote copies, remote signals or barrier semaphores. Data moves between devices by JAX's collectives and lax.ppermute only.
A program may use at most 64 MiB of HBM per device.

```python
import jax
import jax.numpy as jnp
from jax import lax

HEADS = 12
HEAD_DIM = 128
WIDTH = 1536
TOK_DEV = 128
NOFF = 4
BLOCKS = 8
DILATION_STRIDE = 1
TOKENS = 1024


def common_keys(key):
    drawn = jax.random.normal(jax.random.fold_in(key, 11), (TOKENS, WIDTH), jnp.float32)
    return jnp.clip(drawn, -6.0, 6.0)


def draw_keys(key, part):
    return common_keys(key).astype(jnp.bfloat16)


def draw_queries(key, part):
    drawn = jnp.clip(jax.random.normal(jax.random.fold_in(key, 12), (TOKENS, WIDTH), jnp.float32), -6.0, 6.0)
    return drawn.astype(jnp.bfloat16)


def place_ends(values, key, smallest, high):
    longest = values.shape.index(max(values.shape))
    spots = []
    for shift in (0, 1):
        where = [jax.random.randint(jax.random.fold_in(key, axis), (), 0, length) for axis, length in enumerate(values.shape)]
        where[longest] = (where[longest] + shift) % values.shape[longest]
        spots.append(tuple(where))
    return values.at[spots[0]].set(smallest).at[spots[1]].set(high)


def block_levels(key, extent, pieces, smallest, high):
    factor_of = 1.0
    for dim, shards_of in pieces:
        steps = jax.random.uniform(jax.random.fold_in(jax.random.fold_in(key, 6), dim), (shards_of,), jnp.float32, smallest / len(pieces), high / len(pieces))
        factor_of = factor_of * jnp.repeat(jnp.exp(steps), extent[dim] // shards_of).reshape((-1,) + (1,) * (len(extent) - 1 - dim))
    return factor_of


def noise(own_key, extent, width, reach, shards=(), dtype=jnp.bfloat16):
    values = width * jax.random.normal(own_key, extent, jnp.float32)
    if shards:
        values = values * block_levels(own_key, extent, shards, -0.22, 0.18)
    return jnp.clip(values, -reach, reach).astype(dtype)


def setup_inputs(seed: int = 0) -> dict:
    key_list = jax.random.split(jax.random.key(seed), 7)
    queries = draw_queries(jax.random.fold_in(key_list[6], 71), 0)
    keys = draw_keys(jax.random.fold_in(key_list[6], 71), 0)
    values = noise(key_list[2], (TOKENS, WIDTH), 1.0, 6.0, ((0, 8), (1, 4)))
    d_out = noise(key_list[3], (TOKENS, WIDTH), 1.0, 6.0, ((0, 8), (1, 4)))
    gain = jnp.clip(1.0 + 0.18 * jax.random.normal(key_list[4], (WIDTH,), jnp.float32), 0.1, 1.9)
    blocks_on = place_ends((jax.random.randint(key_list[5], (BLOCKS, NOFF), 0, 4) < 3).astype(jnp.int32), jax.random.fold_in(key_list[5], 1), 0, 1)
    return {"queries": queries, "keys": keys, "values": values, "d_out": d_out, "gain": gain, "blocks_on": blocks_on}


NEG = -1e+30
EPS = 1e-06

def reference(queries, keys, values, d_out, gain, blocks_on):
    f32 = jnp.float32
    scaling = HEAD_DIM ** (-0.5)
    block_offsets = jnp.array([0, -2 * DILATION_STRIDE, -DILATION_STRIDE, DILATION_STRIDE, 2 * DILATION_STRIDE], jnp.int32)
    allowed = jnp.concatenate([jnp.ones((BLOCKS, 1), jnp.int32), blocks_on], axis=1)
    shape4 = (BLOCKS, TOK_DEV, HEADS, HEAD_DIM)
    query4 = queries.reshape(shape4)
    key4 = keys.reshape(shape4)
    value4 = values.reshape(shape4)

    def block_scores(b):
        target = b + block_offsets
        inside = (target >= 0) & (target < BLOCKS)
        usable = inside & (allowed[b] == 1)
        target = jnp.clip(target, 0, BLOCKS - 1).astype(jnp.int32)
        key_rows = key4[target].reshape(5 * TOK_DEV, HEADS, HEAD_DIM)
        value_rows = value4[target].reshape(5 * TOK_DEV, HEADS, HEAD_DIM)
        score = jnp.einsum('qhe,khe->hqk', query4[b].astype(f32), key_rows.astype(f32)) * scaling
        column = jnp.repeat(usable, TOK_DEV)
        return (jnp.where(column[None, None, :], score, NEG), key_rows, value_rows)

    def forward_pass(b):
        score, key_rows, value_rows = block_scores(b)
        peak = lax.optimization_barrier(jnp.max(score, axis=2))
        expo = jnp.exp(score - peak[:, :, None])
        total = lax.optimization_barrier(jnp.sum(expo, axis=2))
        weight_probs = (expo / total[:, :, None]).astype(jnp.bfloat16)
        result = jnp.einsum('hqk,khe->qhe', weight_probs.astype(f32), value_rows.astype(f32))
        return (result.astype(jnp.bfloat16), peak, total)
    attention, peaks, totals = lax.map(forward_pass, jnp.arange(BLOCKS))
    attention_wide = attention.reshape(TOKENS, WIDTH).astype(f32)
    inverse = lax.rsqrt(lax.optimization_barrier(jnp.mean(attention_wide * attention_wide, axis=1)) + EPS)
    out = (attention_wide * inverse[:, None] * gain).astype(jnp.bfloat16)
    gradient_pass = d_out.astype(f32) * gain
    along = lax.optimization_barrier(jnp.sum(gradient_pass * attention_wide, axis=1))
    d_attn = (inverse[:, None] * gradient_pass - attention_wide * inverse[:, None] ** 3 * along[:, None] / WIDTH).astype(jnp.bfloat16)
    attention_grad_4d = d_attn.reshape(shape4)
    deltas = lax.optimization_barrier(jnp.sum(attention_grad_4d.astype(f32) * attention.astype(f32), axis=3))
    deltas = jnp.transpose(deltas, (0, 2, 1))

    def grad_queries(b):
        score, key_rows, value_rows = block_scores(b)
        probs = jnp.exp(score - peaks[b][:, :, None]) / totals[b][:, :, None]
        d_weights = jnp.einsum('qhe,khe->hqk', attention_grad_4d[b].astype(f32), value_rows.astype(f32))
        d_score = (probs * (d_weights - deltas[b][:, :, None])).astype(jnp.bfloat16)
        result = jnp.einsum('hqk,khe->qhe', d_score.astype(f32), key_rows.astype(f32)) * scaling
        return result.astype(jnp.bfloat16)

    def grad_keys(c):
        own_keys = key4[c].astype(f32)
        own_values = value4[c].astype(f32)
        key_sum = jnp.zeros((TOK_DEV, HEADS, HEAD_DIM), f32)
        value_sum = jnp.zeros((TOK_DEV, HEADS, HEAD_DIM), f32)
        for slot_index in range(5):
            source = c - block_offsets[slot_index]
            inside = (source >= 0) & (source < BLOCKS)
            source = jnp.clip(source, 0, BLOCKS - 1).astype(jnp.int32)
            usable = inside & (allowed[source, slot_index] == 1)
            far_queries = query4[source].astype(f32)
            far_grad = attention_grad_4d[source].astype(f32)
            score = jnp.einsum('qhe,khe->hqk', far_queries, own_keys) * scaling
            probs = jnp.exp(score - peaks[source][:, :, None]) / totals[source][:, :, None]
            probs = jnp.where(usable, probs, 0.0)
            d_weights = jnp.einsum('qhe,khe->hqk', far_grad, own_values)
            d_score = (probs * (d_weights - deltas[source][:, :, None])).astype(jnp.bfloat16)
            key_part = jnp.einsum('hqk,qhe->khe', d_score.astype(f32), far_queries) * scaling
            value_part = jnp.einsum('hqk,qhe->khe', probs.astype(jnp.bfloat16).astype(f32), far_grad)
            if slot_index > 0:
                key_part = lax.optimization_barrier(key_part.astype(jnp.bfloat16)).astype(f32)
                value_part = lax.optimization_barrier(value_part.astype(jnp.bfloat16)).astype(f32)
            key_sum = key_sum + key_part
            value_sum = value_sum + value_part
        return (key_sum.astype(jnp.bfloat16), value_sum.astype(jnp.bfloat16))
    d_queries = lax.map(grad_queries, jnp.arange(BLOCKS)).reshape(TOKENS, WIDTH)
    d_keys, d_values = lax.map(grad_keys, jnp.arange(BLOCKS))
    return (out, d_queries, d_keys.reshape(TOKENS, WIDTH), d_values.reshape(TOKENS, WIDTH))
```

```python
import functools

import jax
import jax.numpy as jnp
from jax import lax
from jax.experimental import pallas as pl
from jax.experimental.pallas import tpu as pltpu
from jax.sharding import PartitionSpec as P

HEAD_DIM = 128
NEG = -1e30
EPS = 1e-06
SCALING = HEAD_DIM ** (-0.5)
STAT_ROWS = 16
F32 = jnp.float32
BF16 = jnp.bfloat16
VMEM_BYTES = 24 * 1024 * 1024


def matmul_nt(left, right):
    return lax.dot_general(left, right, (((1,), (1,)), ((), ())), preferred_element_type=F32)


def matmul(left, right):
    return jnp.dot(left, right, preferred_element_type=F32)


def head_slice(h):
    return slice(h * HEAD_DIM, (h + 1) * HEAD_DIM)


def to_lanes(columns, rows):
    lane = lax.broadcasted_iota(jnp.int32, (rows, HEAD_DIM), 1)
    packed = jnp.zeros((rows, HEAD_DIM), F32)
    for i, column in enumerate(columns):
        packed = jnp.where(lane == i, column, packed)
    return packed


def three_parts(row):
    high = row.astype(BF16).astype(F32)
    mid = (row - high).astype(BF16).astype(F32)
    low = row - high - mid
    return [high, mid, low]


def neighbour_flags(flags_ref, spacing, blocks):
    position = lax.axis_index("band")
    flags = []
    for slot, offset in enumerate((-2 * spacing, -spacing, spacing, 2 * spacing)):
        target = position + offset
        flags.append((target >= 0) & (target < blocks) & (flags_ref[0, slot] == 1))
    return flags


def is_even(spacing):
    return lax.rem(lax.div(lax.axis_index("band"), spacing), 2) == 0


def slot_flags(flags_ref, spacing, blocks):
    m2, m1, p1, p2 = neighbour_flags(flags_ref, spacing, blocks)
    even = is_even(spacing)
    partner = jnp.where(even, p1.astype(jnp.int32), m1.astype(jnp.int32)) == 1
    other = jnp.where(even, m1.astype(jnp.int32), p1.astype(jnp.int32)) == 1
    return [None, m2, partner, p2, other]


def masked_scores(q, keys, flags):
    scores = matmul_nt(q, jnp.concatenate(keys, axis=0)) * SCALING
    n = keys[0].shape[0]
    return [
        scores[:, j * n : (j + 1) * n]
        if flag is None
        else jnp.where(flag, scores[:, j * n : (j + 1) * n], NEG)
        for j, flag in enumerate(flags)
    ]


def forward_kernel(
    spacing, blocks, flags_ref, q_ref, g_ref, gain_ref, own, before, partner, after, other,
    attn_ref, cols_ref, stats_ref,
):
    rows = q_ref.shape[0]
    heads = q_ref.shape[1] // HEAD_DIM
    flags = slot_flags(flags_ref, spacing, blocks)
    held = [own, before, partner, after, other]
    square = jnp.zeros((rows, HEAD_DIM), F32)
    along = jnp.zeros((rows, HEAD_DIM), F32)
    peaks, inverse_totals = [], []
    for h in range(heads):
        sl = head_slice(h)
        scores = masked_scores(q_ref[:, sl], [r[0, :, sl] for r in held], flags)
        peak = functools.reduce(jnp.maximum, scores)
        peak = jnp.max(peak, axis=1, keepdims=True)
        exps = [jnp.exp(s - peak) for s in scores]
        total = jnp.sum(functools.reduce(jnp.add, exps), axis=1, keepdims=True)
        inverse_total = 1.0 / total
        weights = [(e * inverse_total).astype(BF16) for e in exps]
        attn = matmul(
            jnp.concatenate(weights, axis=1),
            jnp.concatenate([r[1, :, sl] for r in held], axis=0),
        ).astype(BF16)
        attn_ref[:, sl] = attn
        wide = attn.astype(F32)
        square = square + wide * wide
        along = along + g_ref[:, sl].astype(F32) * gain_ref[:, sl] * wide
        peaks.append(peak)
        inverse_totals.append(inverse_total)
    cols = to_lanes(
        peaks
        + inverse_totals
        + [jnp.sum(square, axis=1, keepdims=True), jnp.sum(along, axis=1, keepdims=True)],
        rows,
    )
    cols_ref[...] = cols
    stats_ref[...] = cols.T[: stats_ref.shape[0]]


def message_kernel(
    width, n_parts, *refs
):
    flags_ref, attn_ref, g_ref, gain_ref = refs[:4]
    part_refs = refs[4 : 4 + n_parts]
    msg_ref, cols_ref = refs[4 + n_parts :]
    rows = attn_ref.shape[0]
    heads = attn_ref.shape[1] // HEAD_DIM
    own = part_refs[0][...]
    total = functools.reduce(jnp.add, [r[...] for r in part_refs])
    square = total[2 * heads : 2 * heads + 1]
    along = total[2 * heads + 1 : 2 * heads + 2]
    inverse = lax.rsqrt(square / width + EPS)
    second = inverse * inverse * inverse * along / width
    sub = lax.broadcasted_iota(jnp.int32, (HEAD_DIM, rows), 0)
    packed = jnp.where(sub == 0, inverse, jnp.where(sub == 1, second, 0.0)).T
    inverse_col = packed[:, 0:1]
    second_col = packed[:, 1:2]
    deltas = []
    for h in range(heads):
        sl = head_slice(h)
        wide = attn_ref[:, sl].astype(F32)
        d_attn = (
            inverse_col * (g_ref[:, sl].astype(F32) * gain_ref[:, sl]) - wide * second_col
        ).astype(BF16)
        msg_ref[:rows, sl] = d_attn
        deltas.append(jnp.sum(d_attn.astype(F32) * wide, axis=1, keepdims=True))
    cols = to_lanes(deltas + [inverse_col], rows)
    cols_ref[...] = cols
    delta_rows = cols.T
    sub16 = lax.broadcasted_iota(jnp.int32, (STAT_ROWS, rows), 0)
    for h in range(heads):
        lines = (
            three_parts(own[h : h + 1])
            + three_parts(own[heads + h : heads + h + 1])
            + three_parts(delta_rows[h : h + 1])
        )
        block = jnp.zeros((STAT_ROWS, rows), F32)
        for i, line in enumerate(lines):
            block = jnp.where(sub16 == i, line, block)
        for slot in range(4):
            on = jnp.where(flags_ref[0, slot] == 1, 1.0, 0.0)
            block = jnp.where(sub16 == len(lines) + slot, on, block)
        msg_ref[rows:, head_slice(h)] = block.astype(BF16)


def query_kernel(
    spacing, blocks, flags_ref, q_ref, gain_ref, attn_ref, msg_ref, cols_ref, cols2_ref,
    own, before, partner, after, other, out_ref, dq_ref,
):
    rows = q_ref.shape[0]
    heads = q_ref.shape[1] // HEAD_DIM
    flags = slot_flags(flags_ref, spacing, blocks)
    held = [own, before, partner, after, other]
    inverse = cols2_ref[:, heads : heads + 1]
    for h in range(heads):
        sl = head_slice(h)
        out_ref[:, sl] = (attn_ref[:, sl].astype(F32) * inverse * gain_ref[:, sl]).astype(BF16)
        keys = [r[0, :, sl] for r in held]
        scores = masked_scores(q_ref[:, sl], keys, flags)
        peak = cols_ref[:, h : h + 1]
        inverse_total = cols_ref[:, heads + h : heads + h + 1]
        delta = cols2_ref[:, h : h + 1]
        d_weights = matmul_nt(
            msg_ref[:rows, sl], jnp.concatenate([r[1, :, sl] for r in held], axis=0)
        )
        d_scores = [
            (jnp.exp(s - peak) * inverse_total * (d_weights[:, j * rows : (j + 1) * rows] - delta)).astype(BF16)
            for j, s in enumerate(scores)
        ]
        dq = matmul(jnp.concatenate(d_scores, axis=1), jnp.concatenate(keys, axis=0)) * SCALING
        dq_ref[:, sl] = dq.astype(BF16)


def key_kernel(
    spacing, own_ref, q0, q1, q2, q3, q4, m0, m1, m2, m3, m4, dk_ref, dv_ref
):
    rows = own_ref.shape[1]
    heads = own_ref.shape[2] // HEAD_DIM
    even = is_even(spacing)
    q_refs = [q0, q1, q2, q3, q4]
    m_refs = [m0, m1, m2, m3, m4]
    for h in range(heads):
        sl = head_slice(h)
        queries = jnp.concatenate([r[:, sl] for r in q_refs], axis=0)
        d_attn = jnp.concatenate([r[:rows, sl] for r in m_refs], axis=0)
        scores = matmul_nt(own_ref[0, :, sl], queries) * SCALING
        d_weights = matmul_nt(own_ref[1, :, sl], d_attn)
        weights, d_scores = [], []
        for j, m_ref in enumerate(m_refs):
            stats = m_ref[rows:, sl].astype(F32)
            peak = stats[0:1] + stats[1:2] + stats[2:3]
            inverse_total = stats[3:4] + stats[4:5] + stats[5:6]
            delta = stats[6:7] + stats[7:8] + stats[8:9]
            score = scores[:, j * rows : (j + 1) * rows]
            if j > 0:
                f_m2, f_m1, f_p1, f_p2 = [stats[9 + i : 10 + i] for i in range(4)]
                flag = [
                    None,
                    f_p2,
                    jnp.where(even, f_m1, f_p1),
                    f_m2,
                    jnp.where(even, f_p1, f_m1),
                ][j]
                score = jnp.where(flag > 0.5, score, NEG)
            weight = jnp.exp(score - peak) * inverse_total
            weights.append(weight.astype(BF16))
            d_scores.append(
                (weight * (d_weights[:, j * rows : (j + 1) * rows] - delta)).astype(BF16)
            )
        dv_ref[:, sl] = matmul(jnp.concatenate(weights, axis=1), d_attn).astype(BF16)
        dk_ref[:, sl] = (matmul(jnp.concatenate(d_scores, axis=1), queries) * SCALING).astype(BF16)


def call(kernel, name, out_shape, args, smem_first=True):
    specs = [pl.BlockSpec(memory_space=pltpu.VMEM) for _ in args]
    if smem_first:
        specs[0] = pl.BlockSpec(memory_space=pltpu.SMEM)
    return pl.pallas_call(
        kernel,
        name=name,
        out_shape=out_shape,
        in_specs=specs,
        out_specs=jax.tree.map(lambda _: pl.BlockSpec(memory_space=pltpu.VMEM), out_shape),
        compiler_params=pltpu.CompilerParams(vmem_limit_bytes=VMEM_BYTES),
    )(*args)


def moves(blocks, spacing):
    def shift(by):
        return [(i, i + by) for i in range(blocks) if 0 <= i + by < blocks]

    swap = [
        (i, i + spacing if (i // spacing) % 2 == 0 else i - spacing) for i in range(blocks)
    ]
    return shift(2 * spacing), shift(-2 * spacing), swap


def exchange(array, even, blocks, spacing):
    up, down, swap = moves(blocks, spacing)
    before = lax.ppermute(array, "band", up)
    after = lax.ppermute(array, "band", down)
    partner = lax.ppermute(array, "band", swap)
    other = lax.ppermute(lax.select(even, after, before), "band", swap)
    return before, partner, after, other


def local(queries, keys, values, d_out, gain, blocks_on):
    rows, width_here = queries.shape
    blocks = lax.axis_size("band")
    head_devices = lax.axis_size("head")
    spacing = blocks // 8
    width = width_here * head_devices
    even = is_even(spacing)
    gain = gain[None, :]
    shape = jax.ShapeDtypeStruct

    key_value = jnp.stack([keys, values])
    kv = (key_value,) + exchange(key_value, even, blocks, spacing)
    qs = (queries,) + exchange(queries, even, blocks, spacing)

    attn, cols, stats = call(
        functools.partial(forward_kernel, spacing, blocks),
        "attention",
        (
            shape((rows, width_here), BF16),
            shape((rows, HEAD_DIM), F32),
            shape((8, HEAD_DIM), F32),
        ),
        (blocks_on, queries, d_out, gain) + kv,
    )
    parts = [stats]
    for k in range(1, head_devices):
        pairs = [(i, (i + k) % head_devices) for i in range(head_devices)]
        parts.append(lax.ppermute(stats, "head", pairs))
    msg, cols2 = call(
        functools.partial(message_kernel, width, head_devices),
        "attention_gradient",
        (shape((rows + STAT_ROWS, width_here), BF16), shape((rows, HEAD_DIM), F32)),
        (blocks_on, attn, d_out, gain) + tuple(parts),
    )
    msgs = (msg,) + exchange(msg, even, blocks, spacing)
    out, d_queries = call(
        functools.partial(query_kernel, spacing, blocks),
        "query_gradient",
        (shape((rows, width_here), BF16),) * 2,
        (blocks_on, queries, gain, attn, msg, cols, cols2) + kv,
    )
    d_keys, d_values = call(
        functools.partial(key_kernel, spacing),
        "key_gradient",
        (shape((rows, width_here), BF16),) * 2,
        (key_value,) + qs + msgs,
        smem_first=False,
    )
    return out, d_queries, d_keys, d_values


def solution(mesh):
    in_specs = (
        P("band", "head"),
        P("band", "head"),
        P("band", "head"),
        P("band", "head"),
        P("head"),
        P("band", None),
    )
    out_specs = (P("band", "head"), P("band", "head"), P("band", "head"), P("band", "head"))
    return jax.shard_map(local, mesh=mesh, in_specs=in_specs, out_specs=out_specs, check_vma=False)
```

```python
import functools

import jax
import jax.numpy as jnp
from jax import lax
from jax.experimental import pallas as pl
from jax.experimental.pallas import tpu as pltpu
from jax.sharding import PartitionSpec as P

HEAD_DIM = 128
NEG = -1e30
EPS = 1e-06
SCALING = HEAD_DIM ** (-0.5)
STAT_ROWS = 16
F32 = jnp.float32
BF16 = jnp.bfloat16
VMEM_BYTES = 24 * 1024 * 1024


def matmul_nt(left, right):
    return lax.dot_general(left, right, (((1,), (1,)), ((), ())), preferred_element_type=F32)


def matmul(left, right):
    return jnp.dot(left, right, preferred_element_type=F32)


def head_slice(h):
    return slice(h * HEAD_DIM, (h + 1) * HEAD_DIM)


def to_lanes(columns, rows):
    lane = lax.broadcasted_iota(jnp.int32, (rows, HEAD_DIM), 1)
    packed = jnp.zeros((rows, HEAD_DIM), F32)
    for i, column in enumerate(columns):
        packed = jnp.where(lane == i, column, packed)
    return packed


def three_parts(row):
    high = row.astype(BF16).astype(F32)
    mid = (row - high).astype(BF16).astype(F32)
    low = row - high - mid
    return [high, mid, low]


def neighbour_flags(flags_ref, spacing, blocks):
    position = lax.axis_index("band")
    flags = []
    for slot, offset in enumerate((-2 * spacing, -spacing, spacing, 2 * spacing)):
        target = position + offset
        flags.append((target >= 0) & (target < blocks) & (flags_ref[0, slot] == 1))
    return flags


def is_even(spacing):
    return lax.rem(lax.div(lax.axis_index("band"), spacing), 2) == 0


def slot_flags(flags_ref, spacing, blocks):
    m2, m1, p1, p2 = [f.astype(jnp.int32) for f in neighbour_flags(flags_ref, spacing, blocks)]
    even = is_even(spacing)
    pick = lambda if_even, if_odd: jnp.where(even, if_even, if_odd) == 1
    return [None, pick(p1, m1), pick(m1, p1), pick(m2, p2), pick(p2, m2)]


def held_blocks(pack, received, fifth, index, sl):
    return [
        pack[index, :, sl],
        pack[2 + index, :, sl],
        received[index, :, sl],
        received[2 + index, :, sl],
        fifth[index, :, sl],
    ]


def masked_scores(q, keys, flags):
    scores = matmul_nt(q, jnp.concatenate(keys, axis=0)) * SCALING
    n = keys[0].shape[0]
    return [
        scores[:, j * n : (j + 1) * n]
        if flag is None
        else jnp.where(flag, scores[:, j * n : (j + 1) * n], NEG)
        for j, flag in enumerate(flags)
    ]


def forward_kernel(
    spacing, blocks, flags_ref, q_ref, g_ref, gain_ref, pack, received, fifth,
    attn_ref, cols_ref, stats_ref,
):
    rows = q_ref.shape[0]
    heads = q_ref.shape[1] // HEAD_DIM
    flags = slot_flags(flags_ref, spacing, blocks)
    square = jnp.zeros((rows, HEAD_DIM), F32)
    along = jnp.zeros((rows, HEAD_DIM), F32)
    peaks, inverse_totals = [], []
    for h in range(heads):
        sl = head_slice(h)
        scores = masked_scores(
            q_ref[:, sl], held_blocks(pack, received, fifth, 0, sl), flags
        )
        peak = functools.reduce(jnp.maximum, scores)
        peak = jnp.max(peak, axis=1, keepdims=True)
        exps = [jnp.exp(s - peak) for s in scores]
        total = jnp.sum(functools.reduce(jnp.add, exps), axis=1, keepdims=True)
        inverse_total = 1.0 / total
        weights = [(e * inverse_total).astype(BF16) for e in exps]
        attn = matmul(
            jnp.concatenate(weights, axis=1),
            jnp.concatenate(held_blocks(pack, received, fifth, 1, sl), axis=0),
        ).astype(BF16)
        attn_ref[:, sl] = attn
        wide = attn.astype(F32)
        square = square + wide * wide
        along = along + g_ref[:, sl].astype(F32) * gain_ref[:, sl] * wide
        peaks.append(peak)
        inverse_totals.append(inverse_total)
    cols = to_lanes(
        peaks
        + inverse_totals
        + [jnp.sum(square, axis=1, keepdims=True), jnp.sum(along, axis=1, keepdims=True)],
        rows,
    )
    cols_ref[...] = cols
    stats_ref[...] = cols.T[: stats_ref.shape[0]]


def message_kernel(
    width, n_parts, *refs
):
    flags_ref, attn_ref, g_ref, gain_ref = refs[:4]
    part_refs = refs[4 : 4 + n_parts]
    msg_ref, cols_ref = refs[4 + n_parts :]
    rows = attn_ref.shape[0]
    heads = attn_ref.shape[1] // HEAD_DIM
    own = part_refs[0][...]
    total = functools.reduce(jnp.add, [r[...] for r in part_refs])
    square = total[2 * heads : 2 * heads + 1]
    along = total[2 * heads + 1 : 2 * heads + 2]
    inverse = lax.rsqrt(square / width + EPS)
    second = inverse * inverse * inverse * along / width
    sub = lax.broadcasted_iota(jnp.int32, (HEAD_DIM, rows), 0)
    packed = jnp.where(sub == 0, inverse, jnp.where(sub == 1, second, 0.0)).T
    inverse_col = packed[:, 0:1]
    second_col = packed[:, 1:2]
    deltas = []
    for h in range(heads):
        sl = head_slice(h)
        wide = attn_ref[:, sl].astype(F32)
        d_attn = (
            inverse_col * (g_ref[:, sl].astype(F32) * gain_ref[:, sl]) - wide * second_col
        ).astype(BF16)
        msg_ref[:rows, sl] = d_attn
        deltas.append(jnp.sum(d_attn.astype(F32) * wide, axis=1, keepdims=True))
    cols = to_lanes(deltas + [inverse_col], rows)
    cols_ref[...] = cols
    delta_rows = cols.T
    sub16 = lax.broadcasted_iota(jnp.int32, (STAT_ROWS, rows), 0)
    for h in range(heads):
        lines = (
            three_parts(own[h : h + 1])
            + three_parts(own[heads + h : heads + h + 1])
            + three_parts(delta_rows[h : h + 1])
        )
        block = jnp.zeros((STAT_ROWS, rows), F32)
        for i, line in enumerate(lines):
            block = jnp.where(sub16 == i, line, block)
        for slot in range(4):
            on = jnp.where(flags_ref[0, slot] == 1, 1.0, 0.0)
            block = jnp.where(sub16 == len(lines) + slot, on, block)
        msg_ref[rows:, head_slice(h)] = block.astype(BF16)


def query_kernel(
    spacing, blocks, flags_ref, q_ref, gain_ref, attn_ref, msg_ref, cols_ref, cols2_ref,
    pack, received, fifth, out_ref, dq_ref,
):
    rows = q_ref.shape[0]
    heads = q_ref.shape[1] // HEAD_DIM
    flags = slot_flags(flags_ref, spacing, blocks)
    inverse = cols2_ref[:, heads : heads + 1]
    for h in range(heads):
        sl = head_slice(h)
        out_ref[:, sl] = (attn_ref[:, sl].astype(F32) * inverse * gain_ref[:, sl]).astype(BF16)
        keys = held_blocks(pack, received, fifth, 0, sl)
        scores = masked_scores(q_ref[:, sl], keys, flags)
        peak = cols_ref[:, h : h + 1]
        inverse_total = cols_ref[:, heads + h : heads + h + 1]
        delta = cols2_ref[:, h : h + 1]
        d_weights = matmul_nt(
            msg_ref[:rows, sl],
            jnp.concatenate(held_blocks(pack, received, fifth, 1, sl), axis=0),
        )
        d_scores = [
            (jnp.exp(s - peak) * inverse_total * (d_weights[:, j * rows : (j + 1) * rows] - delta)).astype(BF16)
            for j, s in enumerate(scores)
        ]
        dq = matmul(jnp.concatenate(d_scores, axis=1), jnp.concatenate(keys, axis=0)) * SCALING
        dq_ref[:, sl] = dq.astype(BF16)


def key_kernel(
    spacing, pack, q_pack, q_received, q_fifth, m_pack, m_received, m_fifth, dk_ref, dv_ref
):
    rows = pack.shape[1]
    heads = pack.shape[2] // HEAD_DIM
    even = is_even(spacing)
    q_refs = [q_pack.at[0], q_pack.at[1], q_received.at[0], q_received.at[1], q_fifth]
    m_refs = [m_pack.at[0], m_pack.at[1], m_received.at[0], m_received.at[1], m_fifth]
    for h in range(heads):
        sl = head_slice(h)
        queries = jnp.concatenate([r[:, sl] for r in q_refs], axis=0)
        d_attn = jnp.concatenate([r[:rows, sl] for r in m_refs], axis=0)
        scores = matmul_nt(pack[0, :, sl], queries) * SCALING
        d_weights = matmul_nt(pack[1, :, sl], d_attn)
        weights, d_scores = [], []
        for j, m_ref in enumerate(m_refs):
            stats = m_ref[rows:, sl].astype(F32)
            peak = stats[0:1] + stats[1:2] + stats[2:3]
            inverse_total = stats[3:4] + stats[4:5] + stats[5:6]
            delta = stats[6:7] + stats[7:8] + stats[8:9]
            score = scores[:, j * rows : (j + 1) * rows]
            if j > 0:
                m2, m1, p1, p2 = [stats[9 + i : 10 + i] for i in range(4)]
                if_even, if_odd = [None, (m1, p1), (p1, m1), (p2, m2), (m2, p2)][j]
                score = jnp.where(jnp.where(even, if_even, if_odd) > 0.5, score, NEG)
            weight = jnp.exp(score - peak) * inverse_total
            weights.append(weight.astype(BF16))
            d_scores.append(
                (weight * (d_weights[:, j * rows : (j + 1) * rows] - delta)).astype(BF16)
            )
        dv_ref[:, sl] = matmul(jnp.concatenate(weights, axis=1), d_attn).astype(BF16)
        dk_ref[:, sl] = (matmul(jnp.concatenate(d_scores, axis=1), queries) * SCALING).astype(BF16)


def pack_kernel(k, v, q, partner_k, partner_v, partner_q, pack, q_pack):
    pack[0] = k[...]
    pack[1] = v[...]
    pack[2] = partner_k[...]
    pack[3] = partner_v[...]
    q_pack[0] = q[...]
    q_pack[1] = partner_q[...]


def call(kernel, name, out_shape, args, smem_first=True):
    specs = [pl.BlockSpec(memory_space=pltpu.VMEM) for _ in args]
    if smem_first:
        specs[0] = pl.BlockSpec(memory_space=pltpu.SMEM)
    return pl.pallas_call(
        kernel,
        name=name,
        out_shape=out_shape,
        in_specs=specs,
        out_specs=jax.tree.map(lambda _: pl.BlockSpec(memory_space=pltpu.VMEM), out_shape),
        compiler_params=pltpu.CompilerParams(vmem_limit_bytes=VMEM_BYTES),
    )(*args)


def pairs_of(blocks, spacing):
    partner, near = [], []
    for i in range(blocks):
        odd = (i // spacing) % 2
        partner.append((i, i - spacing if odd else i + spacing))
        j = i + spacing if odd else i - spacing
        if 0 <= j < blocks:
            near.append((i, j))
    return partner, near


def head_sum_parts(stats, devices):
    parts = [stats]
    for k in range(1, devices):
        if devices & (devices - 1) == 0:
            pairs = [(i, i ^ k) for i in range(devices)]
        else:
            pairs = [(i, (i + k) % devices) for i in range(devices)]
        parts.append(lax.ppermute(stats, "head", pairs))
    return parts


def local(queries, keys, values, d_out, gain, blocks_on):
    rows, width_here = queries.shape
    blocks = lax.axis_size("band")
    head_devices = lax.axis_size("head")
    spacing = blocks // 8
    heads = width_here // HEAD_DIM
    width = width_here * head_devices
    gain = gain[None, :]
    shape = jax.ShapeDtypeStruct
    partner_pairs, near_pairs = pairs_of(blocks, spacing)

    def to_partner(array):
        return lax.ppermute(array, "band", partner_pairs)

    def to_near(array):
        return lax.ppermute(array, "band", near_pairs)

    pack, q_pack = call(
        pack_kernel,
        "pack",
        (shape((4, rows, width_here), BF16), shape((2, rows, width_here), BF16)),
        (keys, values, queries, to_partner(keys), to_partner(values), to_partner(queries)),
        smem_first=False,
    )
    received = to_near(pack)
    q_pack, received = lax.optimization_barrier((q_pack, received))
    fifth = to_partner(received[:2])
    q_received = to_near(q_pack)

    attn, cols, stats = call(
        functools.partial(forward_kernel, spacing, blocks),
        "attention",
        (
            shape((rows, width_here), BF16),
            shape((rows, HEAD_DIM), F32),
            shape((2 * heads + 2, HEAD_DIM), F32),
        ),
        (blocks_on, queries, d_out, gain, pack, received, fifth),
    )
    parts = head_sum_parts(stats, head_devices)
    q_received, parts = lax.optimization_barrier((q_received, parts))
    q_fifth = to_partner(q_received[0])
    msg, cols2 = call(
        functools.partial(message_kernel, width, head_devices),
        "attention_gradient",
        (shape((rows + STAT_ROWS, width_here), BF16), shape((rows, HEAD_DIM), F32)),
        (blocks_on, attn, d_out, gain) + tuple(parts),
    )
    m_pack = jnp.stack([msg, to_partner(msg)])
    m_received = to_near(m_pack)
    out, d_queries = call(
        functools.partial(query_kernel, spacing, blocks),
        "query_gradient",
        (shape((rows, width_here), BF16),) * 2,
        (blocks_on, queries, gain, attn, msg, cols, cols2, pack, received, fifth),
    )
    m_received, d_queries = lax.optimization_barrier((m_received, d_queries))
    m_fifth = to_partner(m_received[0])
    d_keys, d_values = call(
        functools.partial(key_kernel, spacing),
        "key_gradient",
        (shape((rows, width_here), BF16),) * 2,
        (pack, q_pack, q_received, q_fifth, m_pack, m_received, m_fifth),
        smem_first=False,
    )
    return out, d_queries, d_keys, d_values


def solution(mesh):
    in_specs = (
        P("band", "head"),
        P("band", "head"),
        P("band", "head"),
        P("band", "head"),
        P("head"),
        P("band", None),
    )
    out_specs = (P("band", "head"), P("band", "head"), P("band", "head"), P("band", "head"))
    return jax.shard_map(local, mesh=mesh, in_specs=in_specs, out_specs=out_specs, check_vma=False)
```

```python
import functools

import jax
import jax.numpy as jnp
from jax import lax
from jax.experimental import pallas as pl
from jax.experimental.pallas import tpu as pltpu
from jax.sharding import PartitionSpec as P

HEAD_DIM = 128
NEG = -1e30
EPS = 1e-06
SCALING = HEAD_DIM ** (-0.5)
STAT_ROWS = 16
F32 = jnp.float32
BF16 = jnp.bfloat16
VMEM_BYTES = 24 * 1024 * 1024


def matmul_nt(left, right):
    return lax.dot_general(left, right, (((1,), (1,)), ((), ())), preferred_element_type=F32)


def matmul(left, right):
    return jnp.dot(left, right, preferred_element_type=F32)


def head_slice(h):
    return slice(h * HEAD_DIM, (h + 1) * HEAD_DIM)


def to_lanes(columns, rows):
    lane = lax.broadcasted_iota(jnp.int32, (rows, HEAD_DIM), 1)
    packed = jnp.zeros((rows, HEAD_DIM), F32)
    for i, column in enumerate(columns):
        packed = jnp.where(lane == i, column, packed)
    return packed


def three_parts(row):
    high = row.astype(BF16).astype(F32)
    mid = (row - high).astype(BF16).astype(F32)
    low = row - high - mid
    return [high, mid, low]


def neighbour_flags(flags_ref, spacing, blocks):
    position = lax.axis_index("band")
    flags = []
    for slot, offset in enumerate((-2 * spacing, -spacing, spacing, 2 * spacing)):
        target = position + offset
        flags.append((target >= 0) & (target < blocks) & (flags_ref[0, slot] == 1))
    return flags


def is_even(spacing):
    step = lax.div(lax.axis_index("band"), spacing)
    return lax.rem(step, 2) == 0, lax.rem(lax.div(step, 2), 2) == 0


def slot_flags(flags_ref, spacing, blocks):
    m2, m1, p1, p2 = [f.astype(jnp.int32) for f in neighbour_flags(flags_ref, spacing, blocks)]
    first, even = is_even(spacing)
    return [
        None,
        jnp.where(first, p1, m1) == 1,
        jnp.where(even, p2, m2) == 1,
        jnp.where(even, m2, p2) == 1,
        jnp.where(first, m1, p1) == 1,
    ]


def masked_scores(q, keys, flags):
    scores = matmul_nt(q, jnp.concatenate(keys, axis=0)) * SCALING
    n = keys[0].shape[0]
    return [
        scores[:, j * n : (j + 1) * n]
        if flag is None
        else jnp.where(flag, scores[:, j * n : (j + 1) * n], NEG)
        for j, flag in enumerate(flags)
    ]


def forward_kernel(
    spacing, blocks, flags_ref, q_ref, g_ref, gain_ref, own, partner, inner, outer, fifth,
    attn_ref, cols_ref, stats_ref,
):
    rows = q_ref.shape[0]
    heads = q_ref.shape[1] // HEAD_DIM
    flags = slot_flags(flags_ref, spacing, blocks)
    held = [own, partner, inner, outer, fifth]
    square = jnp.zeros((rows, HEAD_DIM), F32)
    along = jnp.zeros((rows, HEAD_DIM), F32)
    peaks, inverse_totals = [], []
    for h in range(heads):
        sl = head_slice(h)
        scores = masked_scores(
            q_ref[:, sl], [r[0, :, sl] for r in held], flags
        )
        peak = functools.reduce(jnp.maximum, scores)
        peak = jnp.max(peak, axis=1, keepdims=True)
        exps = [jnp.exp(s - peak) for s in scores]
        total = jnp.sum(functools.reduce(jnp.add, exps), axis=1, keepdims=True)
        inverse_total = 1.0 / total
        weights = [(e * inverse_total).astype(BF16) for e in exps]
        attn = matmul(
            jnp.concatenate(weights, axis=1),
            jnp.concatenate([r[1, :, sl] for r in held], axis=0),
        ).astype(BF16)
        attn_ref[:, sl] = attn
        wide = attn.astype(F32)
        square = square + wide * wide
        along = along + g_ref[:, sl].astype(F32) * gain_ref[:, sl] * wide
        peaks.append(peak)
        inverse_totals.append(inverse_total)
    cols = to_lanes(
        peaks
        + inverse_totals
        + [jnp.sum(square, axis=1, keepdims=True), jnp.sum(along, axis=1, keepdims=True)],
        rows,
    )
    cols_ref[...] = cols
    stats_ref[...] = cols.T[: stats_ref.shape[0]]


def message_kernel(
    width, n_parts, *refs
):
    flags_ref, attn_ref, g_ref, gain_ref = refs[:4]
    part_refs = refs[4 : 4 + n_parts]
    msg_ref, cols_ref = refs[4 + n_parts :]
    rows = attn_ref.shape[0]
    heads = attn_ref.shape[1] // HEAD_DIM
    own = part_refs[0][...]
    total = functools.reduce(jnp.add, [r[...] for r in part_refs])
    square = total[2 * heads : 2 * heads + 1]
    along = total[2 * heads + 1 : 2 * heads + 2]
    inverse = lax.rsqrt(square / width + EPS)
    second = inverse * inverse * inverse * along / width
    sub = lax.broadcasted_iota(jnp.int32, (HEAD_DIM, rows), 0)
    packed = jnp.where(sub == 0, inverse, jnp.where(sub == 1, second, 0.0)).T
    inverse_col = packed[:, 0:1]
    second_col = packed[:, 1:2]
    deltas = []
    for h in range(heads):
        sl = head_slice(h)
        wide = attn_ref[:, sl].astype(F32)
        d_attn = (
            inverse_col * (g_ref[:, sl].astype(F32) * gain_ref[:, sl]) - wide * second_col
        ).astype(BF16)
        msg_ref[:rows, sl] = d_attn
        deltas.append(jnp.sum(d_attn.astype(F32) * wide, axis=1, keepdims=True))
    cols = to_lanes(deltas + [inverse_col], rows)
    cols_ref[...] = cols
    delta_rows = cols.T
    sub16 = lax.broadcasted_iota(jnp.int32, (STAT_ROWS, rows), 0)
    for h in range(heads):
        lines = (
            three_parts(own[h : h + 1])
            + three_parts(own[heads + h : heads + h + 1])
            + three_parts(delta_rows[h : h + 1])
        )
        block = jnp.zeros((STAT_ROWS, rows), F32)
        for i, line in enumerate(lines):
            block = jnp.where(sub16 == i, line, block)
        for slot in range(4):
            on = jnp.where(flags_ref[0, slot] == 1, 1.0, 0.0)
            block = jnp.where(sub16 == len(lines) + slot, on, block)
        msg_ref[rows:, head_slice(h)] = block.astype(BF16)


def query_kernel(
    spacing, blocks, flags_ref, q_ref, gain_ref, attn_ref, msg_ref, cols_ref, cols2_ref,
    own, partner, inner, outer, fifth, out_ref, dq_ref,
):
    rows = q_ref.shape[0]
    heads = q_ref.shape[1] // HEAD_DIM
    flags = slot_flags(flags_ref, spacing, blocks)
    held = [own, partner, inner, outer, fifth]
    inverse = cols2_ref[:, heads : heads + 1]
    for h in range(heads):
        sl = head_slice(h)
        out_ref[:, sl] = (attn_ref[:, sl].astype(F32) * inverse * gain_ref[:, sl]).astype(BF16)
        keys = [r[0, :, sl] for r in held]
        scores = masked_scores(q_ref[:, sl], keys, flags)
        peak = cols_ref[:, h : h + 1]
        inverse_total = cols_ref[:, heads + h : heads + h + 1]
        delta = cols2_ref[:, h : h + 1]
        d_weights = matmul_nt(
            msg_ref[:rows, sl],
            jnp.concatenate([r[1, :, sl] for r in held], axis=0),
        )
        d_scores = [
            (jnp.exp(s - peak) * inverse_total * (d_weights[:, j * rows : (j + 1) * rows] - delta)).astype(BF16)
            for j, s in enumerate(scores)
        ]
        dq = matmul(jnp.concatenate(d_scores, axis=1), jnp.concatenate(keys, axis=0)) * SCALING
        dq_ref[:, sl] = dq.astype(BF16)


def key_kernel(spacing, own, q0, q1, q2, q3, q4, m0, m1, m2, m3, m4, dk_ref, dv_ref):
    rows = own.shape[1]
    heads = own.shape[2] // HEAD_DIM
    first, even = is_even(spacing)
    q_refs = [q0, q1, q2, q3, q4]
    m_refs = [m0, m1, m2, m3, m4]
    for h in range(heads):
        sl = head_slice(h)
        queries = jnp.concatenate([r[:, sl] for r in q_refs], axis=0)
        d_attn = jnp.concatenate([r[:rows, sl] for r in m_refs], axis=0)
        scores = matmul_nt(own[0, :, sl], queries) * SCALING
        d_weights = matmul_nt(own[1, :, sl], d_attn)
        weights, d_scores = [], []
        for j, m_ref in enumerate(m_refs):
            stats = m_ref[rows:, sl].astype(F32)
            peak = stats[0:1] + stats[1:2] + stats[2:3]
            inverse_total = stats[3:4] + stats[4:5] + stats[5:6]
            delta = stats[6:7] + stats[7:8] + stats[8:9]
            score = scores[:, j * rows : (j + 1) * rows]
            if j > 0:
                at_m2, at_m1, at_p1, at_p2 = [stats[9 + i : 10 + i] for i in range(4)]
                flag = [
                    None,
                    jnp.where(first, at_m1, at_p1),
                    jnp.where(even, at_m2, at_p2),
                    jnp.where(even, at_p2, at_m2),
                    jnp.where(first, at_p1, at_m1),
                ][j]
                score = jnp.where(flag > 0.5, score, NEG)
            weight = jnp.exp(score - peak) * inverse_total
            weights.append(weight.astype(BF16))
            d_scores.append(
                (weight * (d_weights[:, j * rows : (j + 1) * rows] - delta)).astype(BF16)
            )
        dv_ref[:, sl] = matmul(jnp.concatenate(weights, axis=1), d_attn).astype(BF16)
        dk_ref[:, sl] = (matmul(jnp.concatenate(d_scores, axis=1), queries) * SCALING).astype(BF16)


def call(kernel, name, out_shape, args, smem_first=True):
    specs = [pl.BlockSpec(memory_space=pltpu.VMEM) for _ in args]
    if smem_first:
        specs[0] = pl.BlockSpec(memory_space=pltpu.SMEM)
    return pl.pallas_call(
        kernel,
        name=name,
        out_shape=out_shape,
        in_specs=specs,
        out_specs=jax.tree.map(lambda _: pl.BlockSpec(memory_space=pltpu.VMEM), out_shape),
        compiler_params=pltpu.CompilerParams(vmem_limit_bytes=VMEM_BYTES),
    )(*args)


def pairs_of(blocks, spacing):
    partner, inner, outer = [], [], []
    for i in range(blocks):
        step = i // spacing
        partner.append((i, i + spacing if step % 2 == 0 else i - spacing))
        to = 2 * spacing if (step // 2) % 2 == 0 else -2 * spacing
        if 0 <= i + to < blocks:
            inner.append((i, i + to))
        if 0 <= i - to < blocks:
            outer.append((i, i - to))
    return partner, inner, outer


def head_sum_parts(stats, devices):
    parts = [stats]
    for k in range(1, devices):
        if devices & (devices - 1) == 0:
            pairs = [(i, i ^ k) for i in range(devices)]
        else:
            pairs = [(i, (i + k) % devices) for i in range(devices)]
        parts.append(lax.ppermute(stats, "head", pairs))
    return parts


def local(queries, keys, values, d_out, gain, blocks_on):
    rows, width_here = queries.shape
    blocks = lax.axis_size("band")
    head_devices = lax.axis_size("head")
    spacing = blocks // 8
    heads = width_here // HEAD_DIM
    width = width_here * head_devices
    gain = gain[None, :]
    shape = jax.ShapeDtypeStruct
    partner_pairs, inner_pairs, outer_pairs = pairs_of(blocks, spacing)
    first, even = is_even(spacing)

    def swaps(array):
        outer = lax.ppermute(array, "band", outer_pairs)
        inner = lax.ppermute(array, "band", inner_pairs)
        return array, lax.ppermute(array, "band", partner_pairs), inner, outer

    def with_fifth(held):
        passed = lax.select(first == even, held[2], held[3])
        return tuple(held) + (lax.ppermute(passed, "band", partner_pairs),)

    kv = swaps(jnp.stack([keys, values]))
    qs = swaps(queries)
    kv = with_fifth(kv)

    attn, cols, stats = call(
        functools.partial(forward_kernel, spacing, blocks),
        "attention",
        (
            shape((rows, width_here), BF16),
            shape((rows, HEAD_DIM), F32),
            shape((2 * heads + 2, HEAD_DIM), F32),
        ),
        (blocks_on, queries, d_out, gain) + kv,
    )
    parts = head_sum_parts(stats, head_devices)
    qs, parts = lax.optimization_barrier((qs, parts))
    qs = with_fifth(qs)
    msg, cols2 = call(
        functools.partial(message_kernel, width, head_devices),
        "attention_gradient",
        (shape((rows + STAT_ROWS, width_here), BF16), shape((rows, HEAD_DIM), F32)),
        (blocks_on, attn, d_out, gain) + tuple(parts),
    )
    msgs = swaps(msg)
    out, d_queries = call(
        functools.partial(query_kernel, spacing, blocks),
        "query_gradient",
        (shape((rows, width_here), BF16),) * 2,
        (blocks_on, queries, gain, attn, msg, cols, cols2) + kv,
    )
    msgs, d_queries = lax.optimization_barrier((msgs, d_queries))
    msgs = with_fifth(msgs)
    d_keys, d_values = call(
        functools.partial(key_kernel, spacing),
        "key_gradient",
        (shape((rows, width_here), BF16),) * 2,
        (kv[0],) + qs + msgs,
        smem_first=False,
    )
    return out, d_queries, d_keys, d_values


def solution(mesh):
    in_specs = (
        P("band", "head"),
        P("band", "head"),
        P("band", "head"),
        P("band", "head"),
        P("head"),
        P("band", None),
    )
    out_specs = (P("band", "head"), P("band", "head"), P("band", "head"), P("band", "head"))
    return jax.shard_map(local, mesh=mesh, in_specs=in_specs, out_specs=out_specs, check_vma=False)
```

```python
import functools

import jax
import jax.numpy as jnp
from jax import lax
from jax.experimental import pallas as pl
from jax.experimental.pallas import tpu as pltpu
from jax.sharding import PartitionSpec as P

HEAD_DIM = 128
NEG = -1e30
EPS = 1e-06
SCALING = HEAD_DIM ** (-0.5)
STAT_ROWS = 16
F32 = jnp.float32
BF16 = jnp.bfloat16
VMEM_BYTES = 24 * 1024 * 1024


def matmul_nt(left, right):
    return lax.dot_general(left, right, (((1,), (1,)), ((), ())), preferred_element_type=F32)


def matmul(left, right):
    return jnp.dot(left, right, preferred_element_type=F32)


def head_slice(h):
    return slice(h * HEAD_DIM, (h + 1) * HEAD_DIM)


def to_lanes(columns, rows):
    lane = lax.broadcasted_iota(jnp.int32, (rows, HEAD_DIM), 1)
    packed = jnp.zeros((rows, HEAD_DIM), F32)
    for i, column in enumerate(columns):
        packed = jnp.where(lane == i, column, packed)
    return packed


def three_parts(row):
    high = row.astype(BF16).astype(F32)
    mid = (row - high).astype(BF16).astype(F32)
    low = row - high - mid
    return [high, mid, low]


def neighbour_flags(flags_ref, spacing, blocks):
    position = lax.axis_index("band")
    flags = []
    for slot, offset in enumerate((-2 * spacing, -spacing, spacing, 2 * spacing)):
        target = position + offset
        flags.append((target >= 0) & (target < blocks) & (flags_ref[0, slot] == 1))
    return flags


def is_even(spacing):
    step = lax.div(lax.axis_index("band"), spacing)
    return lax.rem(step, 2) == 0, lax.rem(lax.div(step, 2), 2) == 0


def slot_flags(flags_ref, spacing, blocks):
    m2, m1, p1, p2 = [f.astype(jnp.int32) for f in neighbour_flags(flags_ref, spacing, blocks)]
    first, even = is_even(spacing)
    return [
        None,
        jnp.where(even, m2, p2) == 1,
        jnp.where(even, p2, m2) == 1,
        jnp.where(first, p1, m1) == 1,
        jnp.where(first, m1, p1) == 1,
    ]


def masked_scores(q, keys, flags):
    scores = matmul_nt(q, jnp.concatenate(keys, axis=0)) * SCALING
    n = keys[0].shape[0]
    return [
        scores[:, j * n : (j + 1) * n]
        if flag is None
        else jnp.where(flag, scores[:, j * n : (j + 1) * n], NEG)
        for j, flag in enumerate(flags)
    ]


def forward_kernel(
    spacing, blocks, flags_ref, q_ref, g_ref, gain_ref, own, outer, inner, partner, fifth,
    attn_ref, cols_ref, stats_ref,
):
    rows = q_ref.shape[0]
    heads = q_ref.shape[1] // HEAD_DIM
    flags = slot_flags(flags_ref, spacing, blocks)
    held = [own, outer, inner, partner, fifth]
    square = jnp.zeros((rows, HEAD_DIM), F32)
    along = jnp.zeros((rows, HEAD_DIM), F32)
    peaks, inverse_totals = [], []
    for h in range(heads):
        sl = head_slice(h)
        scores = masked_scores(
            q_ref[:, sl], [r[0, :, sl] for r in held], flags
        )
        peak = functools.reduce(jnp.maximum, scores)
        peak = jnp.max(peak, axis=1, keepdims=True)
        exps = [jnp.exp(s - peak) for s in scores]
        total = jnp.sum(functools.reduce(jnp.add, exps), axis=1, keepdims=True)
        inverse_total = 1.0 / total
        weights = [(e * inverse_total).astype(BF16) for e in exps]
        attn = matmul(
            jnp.concatenate(weights, axis=1),
            jnp.concatenate([r[1, :, sl] for r in held], axis=0),
        ).astype(BF16)
        attn_ref[:, sl] = attn
        wide = attn.astype(F32)
        square = square + wide * wide
        along = along + g_ref[:, sl].astype(F32) * gain_ref[:, sl] * wide
        peaks.append(peak)
        inverse_totals.append(inverse_total)
    cols = to_lanes(
        peaks
        + inverse_totals
        + [jnp.sum(square, axis=1, keepdims=True), jnp.sum(along, axis=1, keepdims=True)],
        rows,
    )
    cols_ref[...] = cols
    stats_ref[...] = jnp.broadcast_to(cols.T[None, : stats_ref.shape[1]], stats_ref.shape)


def message_kernel(
    width, flags_ref, attn_ref, g_ref, gain_ref, stats_ref, parts_ref, msg_ref, cols_ref
):
    rows = attn_ref.shape[0]
    heads = attn_ref.shape[1] // HEAD_DIM
    own = stats_ref[0]
    total = jnp.sum(parts_ref[...], axis=0)
    square = total[2 * heads : 2 * heads + 1]
    along = total[2 * heads + 1 : 2 * heads + 2]
    inverse = lax.rsqrt(square / width + EPS)
    second = inverse * inverse * inverse * along / width
    sub = lax.broadcasted_iota(jnp.int32, (HEAD_DIM, rows), 0)
    packed = jnp.where(sub == 0, inverse, jnp.where(sub == 1, second, 0.0)).T
    inverse_col = packed[:, 0:1]
    second_col = packed[:, 1:2]
    deltas = []
    for h in range(heads):
        sl = head_slice(h)
        wide = attn_ref[:, sl].astype(F32)
        d_attn = (
            inverse_col * (g_ref[:, sl].astype(F32) * gain_ref[:, sl]) - wide * second_col
        ).astype(BF16)
        msg_ref[:rows, sl] = d_attn
        deltas.append(jnp.sum(d_attn.astype(F32) * wide, axis=1, keepdims=True))
    cols = to_lanes(deltas + [inverse_col], rows)
    cols_ref[...] = cols
    delta_rows = cols.T
    sub16 = lax.broadcasted_iota(jnp.int32, (STAT_ROWS, rows), 0)
    for h in range(heads):
        lines = (
            three_parts(own[h : h + 1])
            + three_parts(own[heads + h : heads + h + 1])
            + three_parts(delta_rows[h : h + 1])
        )
        block = jnp.zeros((STAT_ROWS, rows), F32)
        for i, line in enumerate(lines):
            block = jnp.where(sub16 == i, line, block)
        for slot in range(4):
            on = jnp.where(flags_ref[0, slot] == 1, 1.0, 0.0)
            block = jnp.where(sub16 == len(lines) + slot, on, block)
        msg_ref[rows:, head_slice(h)] = block.astype(BF16)


def query_kernel(
    spacing, blocks, flags_ref, q_ref, gain_ref, attn_ref, msg_ref, cols_ref, cols2_ref,
    own, outer, inner, partner, fifth, out_ref, dq_ref,
):
    rows = q_ref.shape[0]
    heads = q_ref.shape[1] // HEAD_DIM
    flags = slot_flags(flags_ref, spacing, blocks)
    held = [own, outer, inner, partner, fifth]
    inverse = cols2_ref[:, heads : heads + 1]
    for h in range(heads):
        sl = head_slice(h)
        out_ref[:, sl] = (attn_ref[:, sl].astype(F32) * inverse * gain_ref[:, sl]).astype(BF16)
        keys = [r[0, :, sl] for r in held]
        scores = masked_scores(q_ref[:, sl], keys, flags)
        peak = cols_ref[:, h : h + 1]
        inverse_total = cols_ref[:, heads + h : heads + h + 1]
        delta = cols2_ref[:, h : h + 1]
        d_weights = matmul_nt(
            msg_ref[:rows, sl],
            jnp.concatenate([r[1, :, sl] for r in held], axis=0),
        )
        d_scores = [
            (jnp.exp(s - peak) * inverse_total * (d_weights[:, j * rows : (j + 1) * rows] - delta)).astype(BF16)
            for j, s in enumerate(scores)
        ]
        dq = matmul(jnp.concatenate(d_scores, axis=1), jnp.concatenate(keys, axis=0)) * SCALING
        dq_ref[:, sl] = dq.astype(BF16)


def key_kernel(spacing, own, q0, q1, q2, q3, q4, m0, m1, m2, m3, m4, dk_ref, dv_ref):
    rows = own.shape[1]
    heads = own.shape[2] // HEAD_DIM
    first, even = is_even(spacing)
    q_refs = [q0, q1, q2, q3, q4]
    m_refs = [m0, m1, m2, m3, m4]
    for h in range(heads):
        sl = head_slice(h)
        queries = jnp.concatenate([r[:, sl] for r in q_refs], axis=0)
        d_attn = jnp.concatenate([r[:rows, sl] for r in m_refs], axis=0)
        scores = matmul_nt(own[0, :, sl], queries) * SCALING
        d_weights = matmul_nt(own[1, :, sl], d_attn)
        weights, d_scores = [], []
        for j, m_ref in enumerate(m_refs):
            stats = m_ref[rows:, sl].astype(F32)
            peak = stats[0:1] + stats[1:2] + stats[2:3]
            inverse_total = stats[3:4] + stats[4:5] + stats[5:6]
            delta = stats[6:7] + stats[7:8] + stats[8:9]
            score = scores[:, j * rows : (j + 1) * rows]
            if j > 0:
                at_m2, at_m1, at_p1, at_p2 = [stats[9 + i : 10 + i] for i in range(4)]
                flag = [
                    None,
                    jnp.where(even, at_p2, at_m2),
                    jnp.where(even, at_m2, at_p2),
                    jnp.where(first, at_m1, at_p1),
                    jnp.where(first, at_p1, at_m1),
                ][j]
                score = jnp.where(flag > 0.5, score, NEG)
            weight = jnp.exp(score - peak) * inverse_total
            weights.append(weight.astype(BF16))
            d_scores.append(
                (weight * (d_weights[:, j * rows : (j + 1) * rows] - delta)).astype(BF16)
            )
        dv_ref[:, sl] = matmul(jnp.concatenate(weights, axis=1), d_attn).astype(BF16)
        dk_ref[:, sl] = (matmul(jnp.concatenate(d_scores, axis=1), queries) * SCALING).astype(BF16)


def call(kernel, name, out_shape, args, smem_first=True):
    specs = [pl.BlockSpec(memory_space=pltpu.VMEM) for _ in args]
    if smem_first:
        specs[0] = pl.BlockSpec(memory_space=pltpu.SMEM)
    return pl.pallas_call(
        kernel,
        name=name,
        out_shape=out_shape,
        in_specs=specs,
        out_specs=jax.tree.map(lambda _: pl.BlockSpec(memory_space=pltpu.VMEM), out_shape),
        compiler_params=pltpu.CompilerParams(vmem_limit_bytes=VMEM_BYTES),
    )(*args)


def pairs_of(blocks, spacing):
    partner, inner, outer = [], [], []
    for i in range(blocks):
        step = i // spacing
        partner.append((i, i + spacing if step % 2 == 0 else i - spacing))
        to = 2 * spacing if (step // 2) % 2 == 0 else -2 * spacing
        if 0 <= i + to < blocks:
            inner.append((i, i + to))
        if 0 <= i - to < blocks:
            outer.append((i, i - to))
    return partner, inner, outer


def local(queries, keys, values, d_out, gain, blocks_on):
    rows, width_here = queries.shape
    blocks = lax.axis_size("band")
    head_devices = lax.axis_size("head")
    spacing = blocks // 8
    heads = width_here // HEAD_DIM
    width = width_here * head_devices
    gain = gain[None, :]
    shape = jax.ShapeDtypeStruct
    partner_pairs, inner_pairs, outer_pairs = pairs_of(blocks, spacing)
    first, even = is_even(spacing)

    def swaps(array):
        return (array,) + tuple(
            lax.ppermute(array, "band", pairs)
            for pairs in (outer_pairs, inner_pairs, partner_pairs)
        )

    def with_fifth(held):
        passed = lax.select(first == even, held[2], held[1])
        return tuple(held) + (lax.ppermute(passed, "band", partner_pairs),)

    kv = swaps(jnp.stack([keys, values]))
    qs = swaps(queries)
    kv = with_fifth(kv)

    attn, cols, stats = call(
        functools.partial(forward_kernel, spacing, blocks),
        "attention",
        (
            shape((rows, width_here), BF16),
            shape((rows, HEAD_DIM), F32),
            shape((head_devices, 2 * heads + 2, HEAD_DIM), F32),
        ),
        (blocks_on, queries, d_out, gain) + kv,
    )
    parts = lax.all_to_all(stats, "head", 0, 0)
    qs, parts = lax.optimization_barrier((qs, parts))
    msg, cols2 = call(
        functools.partial(message_kernel, width),
        "attention_gradient",
        (shape((rows + STAT_ROWS, width_here), BF16), shape((rows, HEAD_DIM), F32)),
        (blocks_on, attn, d_out, gain, stats, parts),
    )
    msgs = swaps(msg)
    out, d_queries = call(
        functools.partial(query_kernel, spacing, blocks),
        "query_gradient",
        (shape((rows, width_here), BF16),) * 2,
        (blocks_on, queries, gain, attn, msg, cols, cols2) + kv,
    )
    qs = with_fifth(qs)
    msgs, d_queries, qs = lax.optimization_barrier((msgs, d_queries, qs))
    msgs = with_fifth(msgs)
    d_keys, d_values = call(
        functools.partial(key_kernel, spacing),
        "key_gradient",
        (shape((rows, width_here), BF16),) * 2,
        (kv[0],) + qs + msgs,
        smem_first=False,
    )
    return out, d_queries, d_keys, d_values


def solution(mesh):
    in_specs = (
        P("band", "head"),
        P("band", "head"),
        P("band", "head"),
        P("band", "head"),
        P("head"),
        P("band", None),
    )
    out_specs = (P("band", "head"), P("band", "head"), P("band", "head"), P("band", "head"))
    return jax.shard_map(local, mesh=mesh, in_specs=in_specs, out_specs=out_specs, check_vma=False)
```

```python
import functools

import jax
import jax.numpy as jnp
from jax import lax
from jax.experimental import pallas as pl
from jax.experimental.pallas import tpu as pltpu
from jax.sharding import PartitionSpec as P

HEAD_DIM = 128
NEG = -1e30
EPS = 1e-06
SCALING = HEAD_DIM ** (-0.5)
STAT_ROWS = 16
F32 = jnp.float32
BF16 = jnp.bfloat16
VMEM_BYTES = 24 * 1024 * 1024


def matmul_nt(left, right):
    return lax.dot_general(left, right, (((1,), (1,)), ((), ())), preferred_element_type=F32)


def matmul(left, right):
    return jnp.dot(left, right, preferred_element_type=F32)


def head_slice(h):
    return slice(h * HEAD_DIM, (h + 1) * HEAD_DIM)


def to_lanes(columns, rows):
    lane = lax.broadcasted_iota(jnp.int32, (rows, HEAD_DIM), 1)
    packed = jnp.zeros((rows, HEAD_DIM), F32)
    for i, column in enumerate(columns):
        packed = jnp.where(lane == i, column, packed)
    return packed


def three_parts(row):
    high = row.astype(BF16).astype(F32)
    mid = (row - high).astype(BF16).astype(F32)
    low = row - high - mid
    return [high, mid, low]


def neighbour_flags(flags_ref, spacing, blocks):
    position = lax.axis_index("band")
    flags = []
    for slot, offset in enumerate((-2 * spacing, -spacing, spacing, 2 * spacing)):
        target = position + offset
        flags.append((target >= 0) & (target < blocks) & (flags_ref[0, slot] == 1))
    return flags


def is_even(spacing):
    step = lax.div(lax.axis_index("band"), spacing)
    return lax.rem(step, 2) == 0, lax.rem(lax.div(step, 2), 2) == 0


def far_members(spacing, blocks):
    pair = lax.div(lax.axis_index("band"), 2 * spacing)
    even = lax.rem(pair, 2) == 0
    last = blocks // (2 * spacing) - 1
    outer = jnp.clip(jnp.where(even, pair - 1, pair + 1), 0, last)
    return outer, jnp.clip(jnp.where(even, pair + 1, pair - 1), 0, last)


def slot_flags(flags_ref, spacing, blocks):
    m2, m1, p1, p2 = [f.astype(jnp.int32) for f in neighbour_flags(flags_ref, spacing, blocks)]
    first, even = is_even(spacing)
    return [
        None,
        jnp.where(even, m2, p2) == 1,
        jnp.where(even, p2, m2) == 1,
        jnp.where(first, p1, m1) == 1,
        jnp.where(first, m1, p1) == 1,
    ]


def masked_scores(q, keys, flags):
    scores = matmul_nt(q, jnp.concatenate(keys, axis=0)) * SCALING
    n = keys[0].shape[0]
    return [
        scores[:, j * n : (j + 1) * n]
        if flag is None
        else jnp.where(flag, scores[:, j * n : (j + 1) * n], NEG)
        for j, flag in enumerate(flags)
    ]


def forward_kernel(
    spacing, blocks, flags_ref, q_ref, g_ref, gain_ref, own, gathered, partner, fifth,
    attn_ref, cols_ref, stats_ref,
):
    rows = q_ref.shape[0]
    heads = q_ref.shape[1] // HEAD_DIM
    flags = slot_flags(flags_ref, spacing, blocks)
    outer, inner = far_members(spacing, blocks)
    held = [own, gathered.at[outer], gathered.at[inner], partner, fifth]
    square = jnp.zeros((rows, HEAD_DIM), F32)
    along = jnp.zeros((rows, HEAD_DIM), F32)
    peaks, inverse_totals = [], []
    for h in range(heads):
        sl = head_slice(h)
        scores = masked_scores(
            q_ref[:, sl], [r[0, :, sl] for r in held], flags
        )
        peak = functools.reduce(jnp.maximum, scores)
        peak = jnp.max(peak, axis=1, keepdims=True)
        exps = [jnp.exp(s - peak) for s in scores]
        total = jnp.sum(functools.reduce(jnp.add, exps), axis=1, keepdims=True)
        inverse_total = 1.0 / total
        weights = [(e * inverse_total).astype(BF16) for e in exps]
        attn = matmul(
            jnp.concatenate(weights, axis=1),
            jnp.concatenate([r[1, :, sl] for r in held], axis=0),
        ).astype(BF16)
        attn_ref[:, sl] = attn
        wide = attn.astype(F32)
        square = square + wide * wide
        along = along + g_ref[:, sl].astype(F32) * gain_ref[:, sl] * wide
        peaks.append(peak)
        inverse_totals.append(inverse_total)
    cols = to_lanes(
        peaks
        + inverse_totals
        + [jnp.sum(square, axis=1, keepdims=True), jnp.sum(along, axis=1, keepdims=True)],
        rows,
    )
    cols_ref[...] = cols
    stats_ref[...] = cols.T[: stats_ref.shape[0]]


def message_kernel(
    width, flags_ref, attn_ref, g_ref, gain_ref, stats_ref, parts_ref, msg_ref, cols_ref
):
    rows = attn_ref.shape[0]
    heads = attn_ref.shape[1] // HEAD_DIM
    own = stats_ref[...]
    total = jnp.sum(parts_ref[...], axis=0)
    square = total[2 * heads : 2 * heads + 1]
    along = total[2 * heads + 1 : 2 * heads + 2]
    inverse = lax.rsqrt(square / width + EPS)
    second = inverse * inverse * inverse * along / width
    sub = lax.broadcasted_iota(jnp.int32, (HEAD_DIM, rows), 0)
    packed = jnp.where(sub == 0, inverse, jnp.where(sub == 1, second, 0.0)).T
    inverse_col = packed[:, 0:1]
    second_col = packed[:, 1:2]
    deltas = []
    for h in range(heads):
        sl = head_slice(h)
        wide = attn_ref[:, sl].astype(F32)
        d_attn = (
            inverse_col * (g_ref[:, sl].astype(F32) * gain_ref[:, sl]) - wide * second_col
        ).astype(BF16)
        msg_ref[:rows, sl] = d_attn
        deltas.append(jnp.sum(d_attn.astype(F32) * wide, axis=1, keepdims=True))
    cols = to_lanes(deltas + [inverse_col], rows)
    cols_ref[...] = cols
    delta_rows = cols.T
    sub16 = lax.broadcasted_iota(jnp.int32, (STAT_ROWS, rows), 0)
    for h in range(heads):
        lines = (
            three_parts(own[h : h + 1])
            + three_parts(own[heads + h : heads + h + 1])
            + three_parts(delta_rows[h : h + 1])
        )
        block = jnp.zeros((STAT_ROWS, rows), F32)
        for i, line in enumerate(lines):
            block = jnp.where(sub16 == i, line, block)
        for slot in range(4):
            on = jnp.where(flags_ref[0, slot] == 1, 1.0, 0.0)
            block = jnp.where(sub16 == len(lines) + slot, on, block)
        msg_ref[rows:, head_slice(h)] = block.astype(BF16)


def query_kernel(
    spacing, blocks, flags_ref, q_ref, gain_ref, attn_ref, msg_ref, cols_ref, cols2_ref,
    own, gathered, partner, fifth, out_ref, dq_ref,
):
    rows = q_ref.shape[0]
    heads = q_ref.shape[1] // HEAD_DIM
    flags = slot_flags(flags_ref, spacing, blocks)
    outer, inner = far_members(spacing, blocks)
    held = [own, gathered.at[outer], gathered.at[inner], partner, fifth]
    inverse = cols2_ref[:, heads : heads + 1]
    for h in range(heads):
        sl = head_slice(h)
        out_ref[:, sl] = (attn_ref[:, sl].astype(F32) * inverse * gain_ref[:, sl]).astype(BF16)
        keys = [r[0, :, sl] for r in held]
        scores = masked_scores(q_ref[:, sl], keys, flags)
        peak = cols_ref[:, h : h + 1]
        inverse_total = cols_ref[:, heads + h : heads + h + 1]
        delta = cols2_ref[:, h : h + 1]
        d_weights = matmul_nt(
            msg_ref[:rows, sl],
            jnp.concatenate([r[1, :, sl] for r in held], axis=0),
        )
        d_scores = [
            (jnp.exp(s - peak) * inverse_total * (d_weights[:, j * rows : (j + 1) * rows] - delta)).astype(BF16)
            for j, s in enumerate(scores)
        ]
        dq = matmul(jnp.concatenate(d_scores, axis=1), jnp.concatenate(keys, axis=0)) * SCALING
        dq_ref[:, sl] = dq.astype(BF16)


def key_kernel(spacing, own, q0, q1, q2, q3, q4, m0, m1, m2, m3, m4, dk_ref, dv_ref):
    rows = own.shape[1]
    heads = own.shape[2] // HEAD_DIM
    first, even = is_even(spacing)
    q_refs = [q0, q1, q2, q3, q4]
    m_refs = [m0, m1, m2, m3, m4]
    for h in range(heads):
        sl = head_slice(h)
        queries = jnp.concatenate([r[:, sl] for r in q_refs], axis=0)
        d_attn = jnp.concatenate([r[:rows, sl] for r in m_refs], axis=0)
        scores = matmul_nt(own[0, :, sl], queries) * SCALING
        d_weights = matmul_nt(own[1, :, sl], d_attn)
        weights, d_scores = [], []
        for j, m_ref in enumerate(m_refs):
            stats = m_ref[rows:, sl].astype(F32)
            peak = stats[0:1] + stats[1:2] + stats[2:3]
            inverse_total = stats[3:4] + stats[4:5] + stats[5:6]
            delta = stats[6:7] + stats[7:8] + stats[8:9]
            score = scores[:, j * rows : (j + 1) * rows]
            if j > 0:
                at_m2, at_m1, at_p1, at_p2 = [stats[9 + i : 10 + i] for i in range(4)]
                flag = [
                    None,
                    jnp.where(even, at_m2, at_p2),
                    jnp.where(even, at_p2, at_m2),
                    jnp.where(first, at_m1, at_p1),
                    jnp.where(first, at_p1, at_m1),
                ][j]
                score = jnp.where(flag > 0.5, score, NEG)
            weight = jnp.exp(score - peak) * inverse_total
            weights.append(weight.astype(BF16))
            d_scores.append(
                (weight * (d_weights[:, j * rows : (j + 1) * rows] - delta)).astype(BF16)
            )
        dv_ref[:, sl] = matmul(jnp.concatenate(weights, axis=1), d_attn).astype(BF16)
        dk_ref[:, sl] = (matmul(jnp.concatenate(d_scores, axis=1), queries) * SCALING).astype(BF16)


def call(kernel, name, out_shape, args, smem_first=True):
    specs = [pl.BlockSpec(memory_space=pltpu.VMEM) for _ in args]
    if smem_first:
        specs[0] = pl.BlockSpec(memory_space=pltpu.SMEM)
    return pl.pallas_call(
        kernel,
        name=name,
        out_shape=out_shape,
        in_specs=specs,
        out_specs=jax.tree.map(lambda _: pl.BlockSpec(memory_space=pltpu.VMEM), out_shape),
        compiler_params=pltpu.CompilerParams(vmem_limit_bytes=VMEM_BYTES),
    )(*args)


def pairs_of(blocks, spacing):
    partner, inner, outer = [], [], []
    for i in range(blocks):
        step = i // spacing
        partner.append((i, i + spacing if step % 2 == 0 else i - spacing))
        to = 2 * spacing if (step // 2) % 2 == 0 else -2 * spacing
        if 0 <= i + to < blocks:
            inner.append((i, i + to))
        if 0 <= i - to < blocks:
            outer.append((i, i - to))
    return partner, inner, outer


def local(queries, keys, values, d_out, gain, blocks_on):
    rows, width_here = queries.shape
    blocks = lax.axis_size("band")
    head_devices = lax.axis_size("head")
    spacing = blocks // 8
    heads = width_here // HEAD_DIM
    width = width_here * head_devices
    gain = gain[None, :]
    shape = jax.ShapeDtypeStruct
    partner_pairs, inner_pairs, outer_pairs = pairs_of(blocks, spacing)
    first, even = is_even(spacing)

    def swaps(array):
        return (array,) + tuple(
            lax.ppermute(array, "band", pairs)
            for pairs in (inner_pairs, outer_pairs, partner_pairs)
        )

    def with_fifth(held):
        passed = lax.select(first == even, held[1], held[2])
        return tuple(held) + (lax.ppermute(passed, "band", partner_pairs),)

    key_value = jnp.stack([keys, values])
    same_parity = [
        list(range(i + odd * spacing, blocks, 2 * spacing)) for odd in (0, 1) for i in range(spacing)
    ]
    gathered = lax.all_gather(key_value, "band", axis_index_groups=same_parity)
    partner = lax.ppermute(key_value, "band", partner_pairs)
    pair = lax.div(lax.axis_index("band"), 2 * spacing)
    beyond = jnp.clip(pair + jnp.where(first, 1, -1), 0, len(same_parity[0]) - 1)
    passed = lax.dynamic_index_in_dim(gathered, beyond, 0, keepdims=False)
    kv = (key_value, gathered, partner, lax.ppermute(passed, "band", partner_pairs))
    queries_late, gathered = lax.optimization_barrier((queries, gathered))
    qs = swaps(queries_late)

    attn, cols, stats = call(
        functools.partial(forward_kernel, spacing, blocks),
        "attention",
        (
            shape((rows, width_here), BF16),
            shape((rows, HEAD_DIM), F32),
            shape((2 * heads + 2, HEAD_DIM), F32),
        ),
        (blocks_on, queries, d_out, gain) + kv,
    )
    parts = lax.all_gather(stats, "head")
    qs, parts = lax.optimization_barrier((qs, parts))
    msg, cols2 = call(
        functools.partial(message_kernel, width),
        "attention_gradient",
        (shape((rows + STAT_ROWS, width_here), BF16), shape((rows, HEAD_DIM), F32)),
        (blocks_on, attn, d_out, gain, stats, parts),
    )
    msgs = swaps(msg)
    out, d_queries = call(
        functools.partial(query_kernel, spacing, blocks),
        "query_gradient",
        (shape((rows, width_here), BF16),) * 2,
        (blocks_on, queries, gain, attn, msg, cols, cols2) + kv,
    )
    qs = with_fifth(qs)
    msgs, d_queries, qs = lax.optimization_barrier((msgs, d_queries, qs))
    msgs = with_fifth(msgs)
    d_keys, d_values = call(
        functools.partial(key_kernel, spacing),
        "key_gradient",
        (shape((rows, width_here), BF16),) * 2,
        (kv[0],) + qs + msgs,
        smem_first=False,
    )
    return out, d_queries, d_keys, d_values


def solution(mesh):
    in_specs = (
        P("band", "head"),
        P("band", "head"),
        P("band", "head"),
        P("band", "head"),
        P("head"),
        P("band", None),
    )
    out_specs = (P("band", "head"), P("band", "head"), P("band", "head"), P("band", "head"))
    return jax.shard_map(local, mesh=mesh, in_specs=in_specs, out_specs=out_specs, check_vma=False)
```

```python
import functools

import jax
import jax.numpy as jnp
from jax import lax
from jax.experimental import pallas as pl
from jax.experimental.pallas import tpu as pltpu
from jax.sharding import PartitionSpec as P

HEAD_DIM = 128
NEG = -1e30
EPS = 1e-06
SCALING = HEAD_DIM ** (-0.5)
STAT_ROWS = 16
F32 = jnp.float32
BF16 = jnp.bfloat16
VMEM_BYTES = 24 * 1024 * 1024


def matmul_nt(left, right):
    return lax.dot_general(left, right, (((1,), (1,)), ((), ())), preferred_element_type=F32)


def matmul(left, right):
    return jnp.dot(left, right, preferred_element_type=F32)


def head_slice(h):
    return slice(h * HEAD_DIM, (h + 1) * HEAD_DIM)


def matmul_tn(left, right):
    return lax.dot_general(left, right, (((0,), (0,)), ((), ())), preferred_element_type=F32)


def stack_rows(lines, shape):
    sub = lax.broadcasted_iota(jnp.int32, shape, 0)
    packed = jnp.zeros(shape, F32)
    for i, line in enumerate(lines):
        packed = jnp.where(sub == i, line, packed)
    return packed


def three_parts(row):
    high = row.astype(BF16).astype(F32)
    mid = (row - high).astype(BF16).astype(F32)
    low = row - high - mid
    return [high, mid, low]


def place(spacing):
    step = lax.div(lax.axis_index("band"), spacing)
    return lax.rem(step, 2) == 0, lax.rem(lax.div(step, 2), 2) == 0


def flag_lines(flags_ref, spacing, blocks, shape):
    position = lax.axis_index("band")
    raw, inside = [], []
    for slot, offset in enumerate((-2 * spacing, -spacing, spacing, 2 * spacing)):
        target = position + offset
        on = flags_ref[0, slot] == 1
        raw.append(jnp.where(on, 1.0, 0.0))
        inside.append(jnp.where(on & (target >= 0) & (target < blocks), 1.0, 0.0))
    m2, m1, p1, p2 = inside
    first, even = place(spacing)
    attended = [
        jnp.where(first, p1, m1),
        jnp.where(even, p2, m2),
        jnp.where(even, m2, p2),
        jnp.where(first, m1, p1),
    ]
    return stack_rows(raw + attended, shape)


def raw_scores(q, keys, flags):
    scores = matmul_nt(jnp.concatenate(keys, axis=0), q) * SCALING
    n = keys[0].shape[0]
    parts = [scores[j * n : (j + 1) * n] for j in range(len(keys))]
    return [s if flag is None else jnp.where(flag > 0.5, s, NEG) for s, flag in zip(parts, flags)]


def top(scores):
    return jnp.max(functools.reduce(jnp.maximum, scores), axis=0, keepdims=True)


def total_of(exps):
    return jnp.sum(functools.reduce(jnp.add, exps), axis=0, keepdims=True)


def near_kernel(
    spacing, blocks, flags_ref, q_ref, g_ref, gain_ref, own, inner, partner,
    exps_ref, lines_ref, grad_ref, on_ref,
):
    rows = q_ref.shape[0]
    heads = q_ref.shape[1] // HEAD_DIM
    on_ref[...] = flag_lines(flags_ref, spacing, blocks, on_ref.shape)
    flags = [None, on_ref[4:5], on_ref[5:6]]
    held = [own, partner, inner]
    peaks, totals = [], []
    for h in range(heads):
        sl = head_slice(h)
        scores = raw_scores(q_ref[:, sl], [r[0, :, sl] for r in held], flags)
        peak = top(scores)
        exps = [jnp.exp(s - peak) for s in scores]
        peaks.append(peak)
        totals.append(total_of(exps))
        for j, e in enumerate(exps):
            at = (h * len(held) + j) * rows
            exps_ref[at : at + rows] = e
        grad_ref[sl] = (g_ref[:, sl].astype(F32) * gain_ref[:, sl]).T
    lines_ref[...] = stack_rows(peaks + totals, lines_ref.shape)


def far_kernel(
    q_ref, grad_ref, exps_ref, near_ref, on_ref, own, partner, inner, outer, fifth,
    attn_ref, stats_ref, sums_ref,
):
    heads = q_ref.shape[1] // HEAD_DIM
    near_rows = exps_ref.shape[0] // heads
    flags = [on_ref[6:7], on_ref[7:8]]
    held = [outer, fifth]
    peaks, inverse_totals = [], []
    square = along = 0.0
    for h in range(heads):
        sl = head_slice(h)
        scores = raw_scores(q_ref[:, sl], [r[0, :, sl] for r in held], flags)
        before = near_ref[h : h + 1]
        peak = jnp.maximum(before, top(scores))
        exps = [jnp.exp(s - peak) for s in scores]
        factor = jnp.exp(before - peak)
        inverse_total = 1.0 / (factor * near_ref[heads + h : heads + h + 1] + total_of(exps))
        near = exps_ref[h * near_rows : (h + 1) * near_rows] * (factor * inverse_total)
        weights = [near.astype(BF16)] + [(e * inverse_total).astype(BF16) for e in exps]
        values = [r[1, :, sl] for r in (own, partner, inner, outer, fifth)]
        attn = matmul_tn(jnp.concatenate(values, axis=0), jnp.concatenate(weights, axis=0)).astype(BF16)
        attn_ref[sl] = attn
        wide = attn.astype(F32)
        square = square + wide * wide
        along = along + grad_ref[sl] * wide
        peaks.append(peak)
        inverse_totals.append(inverse_total)
    stats_ref[...] = stack_rows(peaks + inverse_totals, stats_ref.shape)
    sums_ref[...] = stack_rows(
        [jnp.sum(square, axis=0, keepdims=True), jnp.sum(along, axis=0, keepdims=True)],
        sums_ref.shape,
    )


def message_kernel(width, n_parts, *refs):
    on_ref, attn_ref, grad_ref, stats_ref = refs[:4]
    part_refs = refs[4 : 4 + n_parts]
    msg_ref, lines_ref = refs[4 + n_parts :]
    width_here, rows = attn_ref.shape
    heads = width_here // HEAD_DIM
    sums = functools.reduce(jnp.add, [r[...] for r in part_refs])
    inverse = lax.rsqrt(sums[0:1] / width + EPS)
    second = inverse * inverse * inverse * sums[1:2] / width
    line = lambda kind, h: stats_ref[kind * heads + h : kind * heads + h + 1]
    deltas = []
    for h in range(heads):
        sl = head_slice(h)
        attn = attn_ref[sl].astype(F32)
        d_attn = (inverse * grad_ref[sl] - attn * second).astype(BF16)
        msg_ref[sl] = d_attn
        deltas.append(jnp.sum(d_attn.astype(F32) * attn, axis=0, keepdims=True))
    flags = [on_ref[slot : slot + 1] for slot in range(4)]
    for h in range(heads):
        sent = three_parts(line(0, h)) + three_parts(line(1, h)) + three_parts(deltas[h]) + flags
        at = width_here + h * STAT_ROWS
        msg_ref[at : at + STAT_ROWS] = stack_rows(sent, (STAT_ROWS, rows)).astype(BF16)
    lines_ref[...] = stack_rows(deltas + [inverse], lines_ref.shape)


def query_kernel(
    on_ref, q_ref, gain_ref, attn_ref, msg_ref, stats_ref, lines_ref,
    own, partner, inner, outer, fifth, out_ref, dq_ref,
):
    rows = q_ref.shape[0]
    heads = q_ref.shape[1] // HEAD_DIM
    flags = [None] + [on_ref[i : i + 1] for i in range(4, 8)]
    held = [own, partner, inner, outer, fifth]
    inverse = lines_ref[heads : heads + 1]
    for h in range(heads):
        sl = head_slice(h)
        out_ref[:, sl] = ((attn_ref[sl].astype(F32) * inverse).T * gain_ref[:, sl]).astype(BF16)
        keys = [r[0, :, sl] for r in held]
        scores = raw_scores(q_ref[:, sl], keys, flags)
        peak = stats_ref[h : h + 1]
        inverse_total = stats_ref[heads + h : heads + h + 1]
        delta = lines_ref[h : h + 1]
        d_weights = matmul(jnp.concatenate([r[1, :, sl] for r in held], axis=0), msg_ref[sl])
        d_scores = [
            (
                jnp.exp(s - peak)
                * inverse_total
                * (d_weights[j * rows : (j + 1) * rows] - delta)
            ).astype(BF16)
            for j, s in enumerate(scores)
        ]
        dq = matmul_tn(jnp.concatenate(d_scores, axis=0), jnp.concatenate(keys, axis=0))
        dq_ref[:, sl] = (dq * SCALING).astype(BF16)


def key_parts(own, h, q_refs, m_refs, slots, spacing):
    sl = head_slice(h)
    rows, width_here = own.shape[1:]
    first, even = place(spacing)
    queries = jnp.concatenate([r[:, sl] for r in q_refs], axis=0)
    d_attn = jnp.concatenate([r[sl] for r in m_refs], axis=1)
    scores = matmul_nt(own[0, :, sl], queries) * SCALING
    d_weights = matmul(own[1, :, sl], d_attn)
    at = width_here + h * STAT_ROWS
    weights, d_scores = [], []
    for j, (m_ref, slot) in enumerate(zip(m_refs, slots)):
        stats = m_ref[at : at + STAT_ROWS].astype(F32)
        peak = stats[0:1] + stats[1:2] + stats[2:3]
        inverse_total = stats[3:4] + stats[4:5] + stats[5:6]
        delta = stats[6:7] + stats[7:8] + stats[8:9]
        score = scores[:, j * rows : (j + 1) * rows]
        if slot > 0:
            at_m2, at_m1, at_p1, at_p2 = [stats[9 + i : 10 + i] for i in range(4)]
            flag = [
                None,
                jnp.where(first, at_m1, at_p1),
                jnp.where(even, at_m2, at_p2),
                jnp.where(even, at_p2, at_m2),
                jnp.where(first, at_p1, at_m1),
            ][slot]
            score = jnp.where(flag > 0.5, score, NEG)
        weight = jnp.exp(score - peak) * inverse_total
        weights.append(weight.astype(BF16))
        d_scores.append((weight * (d_weights[:, j * rows : (j + 1) * rows] - delta)).astype(BF16))
    d_values = matmul_nt(jnp.concatenate(weights, axis=1), d_attn)
    return matmul(jnp.concatenate(d_scores, axis=1), queries), d_values


def near_key_kernel(spacing, own, q0, q1, q2, q3, m0, m1, m2, m3, dk_ref, dv_ref):
    for h in range(own.shape[2] // HEAD_DIM):
        dk_ref[:, head_slice(h)], dv_ref[:, head_slice(h)] = key_parts(
            own, h, [q0, q1, q2, q3], [m0, m1, m2, m3], (0, 1, 2, 3), spacing
        )


def far_key_kernel(spacing, own, dk_near, dv_near, q4, m4, dk_ref, dv_ref):
    for h in range(own.shape[2] // HEAD_DIM):
        sl = head_slice(h)
        dk, dv = key_parts(own, h, [q4], [m4], (4,), spacing)
        dk_ref[:, sl] = ((dk_near[:, sl] + dk) * SCALING).astype(BF16)
        dv_ref[:, sl] = (dv_near[:, sl] + dv).astype(BF16)


def call(kernel, name, out_shape, args, smem_first=False, cost=None):
    specs = [pl.BlockSpec(memory_space=pltpu.VMEM) for _ in args]
    if smem_first:
        specs[0] = pl.BlockSpec(memory_space=pltpu.SMEM)
    return pl.pallas_call(
        kernel,
        name=name,
        out_shape=out_shape,
        in_specs=specs,
        out_specs=jax.tree.map(lambda _: pl.BlockSpec(memory_space=pltpu.VMEM), out_shape),
        cost_estimate=cost,
        compiler_params=pltpu.CompilerParams(vmem_limit_bytes=VMEM_BYTES),
    )(*args)


def pairs_of(blocks, spacing):
    partner, inner, outer, relay = [], [], [], []
    for i in range(blocks):
        step = i // spacing
        partner.append((i, i + spacing if step % 2 == 0 else i - spacing))
        to = 2 * spacing if (step // 2) % 2 == 0 else -2 * spacing
        if 0 <= i + to < blocks:
            inner.append((i, i + to))
            if 0 <= i + 2 * to < blocks:
                relay.append((i, i + 2 * to))
        if 0 <= i - to < blocks:
            outer.append((i, i - to))
    return partner, inner, outer, relay


def head_sum_parts(sums, devices):
    parts = [sums]
    order = list(range(1, devices))
    for k in order[1:] + order[:1]:
        if devices & (devices - 1) == 0:
            pairs = [(i, i ^ k) for i in range(devices)]
        else:
            pairs = [(i, (i + k) % devices) for i in range(devices)]
        parts.append(lax.ppermute(sums, "head", pairs))
    return parts


def local(queries, keys, values, d_out, gain, blocks_on):
    rows, width_here = queries.shape
    blocks = lax.axis_size("band")
    head_devices = lax.axis_size("head")
    spacing = blocks // 8
    heads = width_here // HEAD_DIM
    width = width_here * head_devices
    gain = gain[None, :]
    partner_pairs, inner_pairs, outer_pairs, relay_pairs = pairs_of(blocks, spacing)
    first, even = place(spacing)

    def wide(lines, dtype=F32):
        return jax.ShapeDtypeStruct((lines, width_here), dtype)

    def narrow(lines, dtype=F32):
        return jax.ShapeDtypeStruct((lines, rows), dtype)

    def to_partner(array):
        return lax.ppermute(array, "band", partner_pairs)

    def swaps(array):
        return [lax.ppermute(array, "band", pairs) for pairs in (inner_pairs, outer_pairs)]

    def passed_on(inner, outer):
        return to_partner(lax.select(first == even, inner, outer))

    own = jnp.stack([keys, values])
    inner, outer = swaps(own)
    partner = to_partner(own)
    q_partner = to_partner(queries)
    exps, near_lines, grad, on = call(
        functools.partial(near_kernel, spacing, blocks),
        "near_attention",
        (narrow(3 * rows * heads), narrow(8), narrow(width_here), narrow(8)),
        (blocks_on, queries, d_out, gain, own, inner, partner),
        smem_first=True,
    )
    exps, q_partner, queries_late = lax.optimization_barrier((exps, q_partner, queries))
    exps, outer = lax.optimization_barrier((exps, outer))
    fifth = passed_on(inner, outer)
    q_inner = lax.ppermute(queries_late, "band", inner_pairs)
    attn, stats, sums = call(
        far_kernel,
        "far_attention",
        (narrow(width_here, BF16), narrow(8), narrow(8)),
        (queries, grad, exps, near_lines, on, own, partner, inner, outer, fifth),
    )
    attn, q_relayed = lax.optimization_barrier((attn, q_inner))
    q_outer = lax.ppermute(q_relayed, "band", relay_pairs)
    parts = head_sum_parts(sums, head_devices)
    q_inner, parts = lax.optimization_barrier((q_inner, parts))
    msg, lines = call(
        functools.partial(message_kernel, width, head_devices),
        "attention_gradient",
        (narrow(width_here + heads * STAT_ROWS, BF16), narrow(8)),
        (on, attn, grad, stats) + tuple(parts),
        cost=pl.CostEstimate(flops=20_000_000_000, bytes_accessed=0, transcendentals=0),
    )
    m_inner, m_outer = swaps(msg)
    m_partner = to_partner(msg)
    out, d_queries = call(
        query_kernel,
        "query_gradient",
        (wide(rows, BF16),) * 2,
        (on, queries, gain, attn, msg, stats, lines, own, partner, inner, outer, fifth),
    )
    q_fifth = passed_on(q_inner, q_outer)
    m_inner, m_outer, m_partner, q_fifth, d_queries = lax.optimization_barrier(
        (m_inner, m_outer, m_partner, q_fifth, d_queries)
    )
    m_fifth = passed_on(m_inner, m_outer)
    dk_near, dv_near = call(
        functools.partial(near_key_kernel, spacing),
        "near_key_gradient",
        (wide(rows),) * 2,
        (own, queries, q_partner, q_inner, q_outer, msg, m_partner, m_inner, m_outer),
    )
    d_keys, d_values = call(
        functools.partial(far_key_kernel, spacing),
        "far_key_gradient",
        (wide(rows, BF16),) * 2,
        (own, dk_near, dv_near, q_fifth, m_fifth),
    )
    return out, d_queries, d_keys, d_values


def solution(mesh):
    in_specs = (
        P("band", "head"),
        P("band", "head"),
        P("band", "head"),
        P("band", "head"),
        P("head"),
        P("band", None),
    )
    out_specs = (P("band", "head"), P("band", "head"), P("band", "head"), P("band", "head"))
    return jax.shard_map(local, mesh=mesh, in_specs=in_specs, out_specs=out_specs, check_vma=False)
```

```python
import functools

import jax
import jax.numpy as jnp
from jax import lax
from jax.experimental import pallas as pl
from jax.experimental.pallas import tpu as pltpu
from jax.sharding import PartitionSpec as P

HEAD_DIM = 128
NEG = -1e30
EPS = 1e-06
SCALING = HEAD_DIM ** (-0.5)
STAT_ROWS = 16
F32 = jnp.float32
BF16 = jnp.bfloat16
VMEM_BYTES = 24 * 1024 * 1024


def matmul_nt(left, right):
    return lax.dot_general(left, right, (((1,), (1,)), ((), ())), preferred_element_type=F32)


def matmul(left, right):
    return jnp.dot(left, right, preferred_element_type=F32)


def head_slice(h):
    return slice(h * HEAD_DIM, (h + 1) * HEAD_DIM)


def matmul_tn(left, right):
    return lax.dot_general(left, right, (((0,), (0,)), ((), ())), preferred_element_type=F32)


def stack_rows(lines, shape):
    sub = lax.broadcasted_iota(jnp.int32, shape, 0)
    packed = jnp.zeros(shape, F32)
    for i, line in enumerate(lines):
        packed = jnp.where(sub == i, line, packed)
    return packed


def three_parts(row):
    high = row.astype(BF16).astype(F32)
    mid = (row - high).astype(BF16).astype(F32)
    low = row - high - mid
    return [high, mid, low]


def place(spacing):
    step = lax.div(lax.axis_index("band"), spacing)
    return lax.rem(step, 2) == 0, lax.rem(lax.div(step, 2), 2) == 0


def flag_lines(flags_ref, spacing, blocks, shape):
    position = lax.axis_index("band")
    raw, inside = [], []
    for slot, offset in enumerate((-2 * spacing, -spacing, spacing, 2 * spacing)):
        target = position + offset
        on = flags_ref[0, slot] == 1
        raw.append(jnp.where(on, 1.0, 0.0))
        inside.append(jnp.where(on & (target >= 0) & (target < blocks), 1.0, 0.0))
    m2, m1, p1, p2 = inside
    first, even = place(spacing)
    attended = [
        jnp.where(first, p1, m1),
        jnp.where(even, p2, m2),
        jnp.where(even, m2, p2),
        jnp.where(first, m1, p1),
    ]
    return stack_rows(raw + attended, shape)


def raw_scores(q, keys, flags):
    scores = matmul_nt(jnp.concatenate(keys, axis=0), q) * SCALING
    n = keys[0].shape[0]
    parts = [scores[j * n : (j + 1) * n] for j in range(len(keys))]
    return [s if flag is None else jnp.where(flag > 0.5, s, NEG) for s, flag in zip(parts, flags)]


def top(scores):
    return jnp.max(functools.reduce(jnp.maximum, scores), axis=0, keepdims=True)


def total_of(exps):
    return jnp.sum(functools.reduce(jnp.add, exps), axis=0, keepdims=True)


def near_kernel(
    spacing, blocks, flags_ref, q_ref, g_ref, gain_ref, own, inner, partner,
    exps_ref, lines_ref, grad_ref, on_ref,
):
    rows = q_ref.shape[0]
    heads = q_ref.shape[1] // HEAD_DIM
    on_ref[...] = flag_lines(flags_ref, spacing, blocks, on_ref.shape)
    flags = [None, on_ref[4:5], on_ref[5:6]]
    held = [own, partner, inner]
    peaks, totals = [], []
    for h in range(heads):
        sl = head_slice(h)
        scores = raw_scores(q_ref[:, sl], [r[0, :, sl] for r in held], flags)
        peak = top(scores)
        exps = [jnp.exp(s - peak) for s in scores]
        peaks.append(peak)
        totals.append(total_of(exps))
        for j, e in enumerate(exps):
            at = (h * len(held) + j) * rows
            exps_ref[at : at + rows] = e
        grad_ref[sl] = (g_ref[:, sl].astype(F32) * gain_ref[:, sl]).T
    lines_ref[...] = stack_rows(peaks + totals, lines_ref.shape)


def mid_kernel(q_ref, near_ref, on_ref, outer, exps_ref, lines_ref):
    rows = q_ref.shape[0]
    heads = q_ref.shape[1] // HEAD_DIM
    peaks, totals, factors = [], [], []
    for h in range(heads):
        sl = head_slice(h)
        (score,) = raw_scores(q_ref[:, sl], [outer[0, :, sl]], [on_ref[6:7]])
        before = near_ref[h : h + 1]
        peak = jnp.maximum(before, top([score]))
        exps = jnp.exp(score - peak)
        factor = jnp.exp(before - peak)
        exps_ref[h * rows : (h + 1) * rows] = exps
        peaks.append(peak)
        totals.append(factor * near_ref[heads + h : heads + h + 1] + total_of([exps]))
        factors.append(factor)
    lines_ref[...] = stack_rows(peaks + totals + factors, lines_ref.shape)


def far_kernel(
    q_ref, grad_ref, exps_ref, outer_exps_ref, mid_ref, on_ref, own, partner, inner, outer, fifth,
    attn_ref, stats_ref, sums_ref,
):
    rows = q_ref.shape[0]
    heads = q_ref.shape[1] // HEAD_DIM
    near_rows = exps_ref.shape[0] // heads
    peaks, inverse_totals = [], []
    square = along = 0.0
    for h in range(heads):
        sl = head_slice(h)
        (score,) = raw_scores(q_ref[:, sl], [fifth[0, :, sl]], [on_ref[7:8]])
        before = mid_ref[h : h + 1]
        peak = jnp.maximum(before, top([score]))
        exps = jnp.exp(score - peak)
        factor = jnp.exp(before - peak)
        inverse_total = 1.0 / (factor * mid_ref[heads + h : heads + h + 1] + total_of([exps]))
        outer_factor = factor * inverse_total
        near_factor = mid_ref[2 * heads + h : 2 * heads + h + 1] * outer_factor
        weights = [
            (exps_ref[h * near_rows : (h + 1) * near_rows] * near_factor).astype(BF16),
            (outer_exps_ref[h * rows : (h + 1) * rows] * outer_factor).astype(BF16),
            (exps * inverse_total).astype(BF16),
        ]
        values = [r[1, :, sl] for r in (own, partner, inner, outer, fifth)]
        attn = matmul_tn(jnp.concatenate(values, axis=0), jnp.concatenate(weights, axis=0)).astype(BF16)
        attn_ref[sl] = attn
        wide = attn.astype(F32)
        square = square + wide * wide
        along = along + grad_ref[sl] * wide
        peaks.append(peak)
        inverse_totals.append(inverse_total)
    stats_ref[...] = stack_rows(peaks + inverse_totals, stats_ref.shape)
    sums_ref[...] = stack_rows(
        [jnp.sum(square, axis=0, keepdims=True), jnp.sum(along, axis=0, keepdims=True)],
        sums_ref.shape,
    )


def message_kernel(width, n_parts, *refs):
    on_ref, attn_ref, grad_ref, stats_ref = refs[:4]
    part_refs = refs[4 : 4 + n_parts]
    msg_ref, lines_ref = refs[4 + n_parts :]
    width_here, rows = attn_ref.shape
    heads = width_here // HEAD_DIM
    sums = functools.reduce(jnp.add, [r[...] for r in part_refs])
    inverse = lax.rsqrt(sums[0:1] / width + EPS)
    second = inverse * inverse * inverse * sums[1:2] / width
    line = lambda kind, h: stats_ref[kind * heads + h : kind * heads + h + 1]
    deltas = []
    for h in range(heads):
        sl = head_slice(h)
        attn = attn_ref[sl].astype(F32)
        d_attn = (inverse * grad_ref[sl] - attn * second).astype(BF16)
        msg_ref[sl] = d_attn
        deltas.append(jnp.sum(d_attn.astype(F32) * attn, axis=0, keepdims=True))
    flags = [on_ref[slot : slot + 1] for slot in range(4)]
    for h in range(heads):
        sent = three_parts(line(0, h)) + three_parts(line(1, h)) + three_parts(deltas[h]) + flags
        at = width_here + h * STAT_ROWS
        msg_ref[at : at + STAT_ROWS] = stack_rows(sent, (STAT_ROWS, rows)).astype(BF16)
    lines_ref[...] = stack_rows(deltas + [inverse], lines_ref.shape)


def query_kernel(
    on_ref, q_ref, gain_ref, attn_ref, msg_ref, stats_ref, lines_ref,
    own, partner, inner, outer, fifth, out_ref, dq_ref,
):
    rows = q_ref.shape[0]
    heads = q_ref.shape[1] // HEAD_DIM
    flags = [None] + [on_ref[i : i + 1] for i in range(4, 8)]
    held = [own, partner, inner, outer, fifth]
    inverse = lines_ref[heads : heads + 1]
    for h in range(heads):
        sl = head_slice(h)
        out_ref[:, sl] = ((attn_ref[sl].astype(F32) * inverse).T * gain_ref[:, sl]).astype(BF16)
        keys = [r[0, :, sl] for r in held]
        scores = raw_scores(q_ref[:, sl], keys, flags)
        peak = stats_ref[h : h + 1]
        inverse_total = stats_ref[heads + h : heads + h + 1]
        delta = lines_ref[h : h + 1]
        d_weights = matmul(jnp.concatenate([r[1, :, sl] for r in held], axis=0), msg_ref[sl])
        d_scores = [
            (
                jnp.exp(s - peak)
                * inverse_total
                * (d_weights[j * rows : (j + 1) * rows] - delta)
            ).astype(BF16)
            for j, s in enumerate(scores)
        ]
        dq = matmul_tn(jnp.concatenate(d_scores, axis=0), jnp.concatenate(keys, axis=0))
        dq_ref[:, sl] = (dq * SCALING).astype(BF16)


def key_parts(own, h, q_refs, m_refs, slots, spacing):
    sl = head_slice(h)
    rows, width_here = own.shape[1:]
    first, even = place(spacing)
    queries = jnp.concatenate([r[:, sl] for r in q_refs], axis=0)
    d_attn = jnp.concatenate([r[sl] for r in m_refs], axis=1)
    scores = matmul_nt(own[0, :, sl], queries) * SCALING
    d_weights = matmul(own[1, :, sl], d_attn)
    at = width_here + h * STAT_ROWS
    weights, d_scores = [], []
    for j, (m_ref, slot) in enumerate(zip(m_refs, slots)):
        stats = m_ref[at : at + STAT_ROWS].astype(F32)
        peak = stats[0:1] + stats[1:2] + stats[2:3]
        inverse_total = stats[3:4] + stats[4:5] + stats[5:6]
        delta = stats[6:7] + stats[7:8] + stats[8:9]
        score = scores[:, j * rows : (j + 1) * rows]
        if slot > 0:
            at_m2, at_m1, at_p1, at_p2 = [stats[9 + i : 10 + i] for i in range(4)]
            flag = [
                None,
                jnp.where(first, at_m1, at_p1),
                jnp.where(even, at_m2, at_p2),
                jnp.where(even, at_p2, at_m2),
                jnp.where(first, at_p1, at_m1),
            ][slot]
            score = jnp.where(flag > 0.5, score, NEG)
        weight = jnp.exp(score - peak) * inverse_total
        weights.append(weight.astype(BF16))
        d_scores.append((weight * (d_weights[:, j * rows : (j + 1) * rows] - delta)).astype(BF16))
    d_values = matmul_nt(jnp.concatenate(weights, axis=1), d_attn)
    return matmul(jnp.concatenate(d_scores, axis=1), queries), d_values


def near_key_kernel(spacing, own, q0, q1, q2, q3, m0, m1, m2, m3, dk_ref, dv_ref):
    for h in range(own.shape[2] // HEAD_DIM):
        dk_ref[:, head_slice(h)], dv_ref[:, head_slice(h)] = key_parts(
            own, h, [q0, q1, q2, q3], [m0, m1, m2, m3], (0, 1, 2, 3), spacing
        )


def far_key_kernel(spacing, own, dk_near, dv_near, q4, m4, dk_ref, dv_ref):
    for h in range(own.shape[2] // HEAD_DIM):
        sl = head_slice(h)
        dk, dv = key_parts(own, h, [q4], [m4], (4,), spacing)
        dk_ref[:, sl] = ((dk_near[:, sl] + dk) * SCALING).astype(BF16)
        dv_ref[:, sl] = (dv_near[:, sl] + dv).astype(BF16)


def call(kernel, name, out_shape, args, smem_first=False, cost=None):
    specs = [pl.BlockSpec(memory_space=pltpu.VMEM) for _ in args]
    if smem_first:
        specs[0] = pl.BlockSpec(memory_space=pltpu.SMEM)
    return pl.pallas_call(
        kernel,
        name=name,
        out_shape=out_shape,
        in_specs=specs,
        out_specs=jax.tree.map(lambda _: pl.BlockSpec(memory_space=pltpu.VMEM), out_shape),
        cost_estimate=cost,
        compiler_params=pltpu.CompilerParams(vmem_limit_bytes=VMEM_BYTES),
    )(*args)


def pairs_of(blocks, spacing):
    partner, inner, outer, relay = [], [], [], []
    for i in range(blocks):
        step = i // spacing
        partner.append((i, i + spacing if step % 2 == 0 else i - spacing))
        to = 2 * spacing if (step // 2) % 2 == 0 else -2 * spacing
        if 0 <= i + to < blocks:
            inner.append((i, i + to))
            if 0 <= i + 2 * to < blocks:
                relay.append((i, i + 2 * to))
        if 0 <= i - to < blocks:
            outer.append((i, i - to))
    return partner, inner, outer, relay


def head_sum_parts(sums, devices):
    parts = [sums]
    order = list(range(1, devices))
    for k in order[1:] + order[:1]:
        if devices & (devices - 1) == 0:
            pairs = [(i, i ^ k) for i in range(devices)]
        else:
            pairs = [(i, (i + k) % devices) for i in range(devices)]
        parts.append(lax.ppermute(sums, "head", pairs))
    return parts


def local(queries, keys, values, d_out, gain, blocks_on):
    rows, width_here = queries.shape
    blocks = lax.axis_size("band")
    head_devices = lax.axis_size("head")
    spacing = blocks // 8
    heads = width_here // HEAD_DIM
    width = width_here * head_devices
    gain = gain[None, :]
    partner_pairs, inner_pairs, outer_pairs, relay_pairs = pairs_of(blocks, spacing)
    first, even = place(spacing)

    def wide(lines, dtype=F32):
        return jax.ShapeDtypeStruct((lines, width_here), dtype)

    def narrow(lines, dtype=F32):
        return jax.ShapeDtypeStruct((lines, rows), dtype)

    def to_partner(array):
        return lax.ppermute(array, "band", partner_pairs)

    def swaps(array):
        return [lax.ppermute(array, "band", pairs) for pairs in (inner_pairs, outer_pairs)]

    def passed_on(inner, outer):
        return to_partner(lax.select(first == even, inner, outer))

    own = jnp.stack([keys, values])
    inner, outer = swaps(own)
    partner = to_partner(own)
    q_partner = to_partner(queries)
    exps, near_lines, grad, on = call(
        functools.partial(near_kernel, spacing, blocks),
        "near_attention",
        (narrow(3 * rows * heads), narrow(8), narrow(width_here), narrow(8)),
        (blocks_on, queries, d_out, gain, own, inner, partner),
        smem_first=True,
    )
    exps, q_partner, queries_late = lax.optimization_barrier((exps, q_partner, queries))
    exps, outer = lax.optimization_barrier((exps, outer))
    fifth = passed_on(inner, outer)
    q_inner = lax.ppermute(queries_late, "band", inner_pairs)
    outer_exps, mid_lines = call(
        mid_kernel,
        "mid_attention",
        (narrow(rows * heads), narrow(STAT_ROWS)),
        (queries, near_lines, on, outer),
    )
    attn, stats, sums = call(
        far_kernel,
        "far_attention",
        (narrow(width_here, BF16), narrow(8), narrow(8)),
        (queries, grad, exps, outer_exps, mid_lines, on, own, partner, inner, outer, fifth),
    )
    attn, q_relayed = lax.optimization_barrier((attn, q_inner))
    q_outer = lax.ppermute(q_relayed, "band", relay_pairs)
    parts = head_sum_parts(sums, head_devices)
    q_inner, parts = lax.optimization_barrier((q_inner, parts))
    msg, lines = call(
        functools.partial(message_kernel, width, head_devices),
        "attention_gradient",
        (narrow(width_here + heads * STAT_ROWS, BF16), narrow(8)),
        (on, attn, grad, stats) + tuple(parts),
        cost=pl.CostEstimate(flops=20_000_000_000, bytes_accessed=0, transcendentals=0),
    )
    m_inner, m_outer = swaps(msg)
    m_partner = to_partner(msg)
    out, d_queries = call(
        query_kernel,
        "query_gradient",
        (wide(rows, BF16),) * 2,
        (on, queries, gain, attn, msg, stats, lines, own, partner, inner, outer, fifth),
    )
    q_fifth = passed_on(q_inner, q_outer)
    m_inner, m_outer, m_partner, q_fifth, d_queries = lax.optimization_barrier(
        (m_inner, m_outer, m_partner, q_fifth, d_queries)
    )
    m_fifth = passed_on(m_inner, m_outer)
    dk_near, dv_near = call(
        functools.partial(near_key_kernel, spacing),
        "near_key_gradient",
        (wide(rows),) * 2,
        (own, queries, q_partner, q_inner, q_outer, msg, m_partner, m_inner, m_outer),
    )
    d_keys, d_values = call(
        functools.partial(far_key_kernel, spacing),
        "far_key_gradient",
        (wide(rows, BF16),) * 2,
        (own, dk_near, dv_near, q_fifth, m_fifth),
    )
    return out, d_queries, d_keys, d_values


def solution(mesh):
    in_specs = (
        P("band", "head"),
        P("band", "head"),
        P("band", "head"),
        P("band", "head"),
        P("head"),
        P("band", None),
    )
    out_specs = (P("band", "head"), P("band", "head"), P("band", "head"), P("band", "head"))
    return jax.shard_map(local, mesh=mesh, in_specs=in_specs, out_specs=out_specs, check_vma=False)
```

```python
import functools

import jax
import jax.numpy as jnp
from jax import lax
from jax.experimental import pallas as pl
from jax.experimental.pallas import tpu as pltpu
from jax.sharding import PartitionSpec as P

HEAD_DIM = 128
NEG = -1e30
EPS = 1e-06
SCALING = HEAD_DIM ** (-0.5)
STAT_ROWS = 16
F32 = jnp.float32
BF16 = jnp.bfloat16
VMEM_BYTES = 24 * 1024 * 1024


def matmul_nt(left, right):
    return lax.dot_general(left, right, (((1,), (1,)), ((), ())), preferred_element_type=F32)


def matmul(left, right):
    return jnp.dot(left, right, preferred_element_type=F32)


def head_slice(h):
    return slice(h * HEAD_DIM, (h + 1) * HEAD_DIM)


def matmul_tn(left, right):
    return lax.dot_general(left, right, (((0,), (0,)), ((), ())), preferred_element_type=F32)


def stack_rows(lines, shape):
    sub = lax.broadcasted_iota(jnp.int32, shape, 0)
    packed = jnp.zeros(shape, F32)
    for i, line in enumerate(lines):
        packed = jnp.where(sub == i, line, packed)
    return packed


def three_parts(row):
    high = row.astype(BF16).astype(F32)
    mid = (row - high).astype(BF16).astype(F32)
    low = row - high - mid
    return [high, mid, low]


def place(spacing):
    step = lax.div(lax.axis_index("band"), spacing)
    return lax.rem(step, 2) == 0, lax.rem(lax.div(step, 2), 2) == 0


def flag_lines(flags_ref, spacing, blocks, shape):
    position = lax.axis_index("band")
    raw, inside = [], []
    for slot, offset in enumerate((-2 * spacing, -spacing, spacing, 2 * spacing)):
        target = position + offset
        on = flags_ref[0, slot] == 1
        raw.append(jnp.where(on, 1.0, 0.0))
        inside.append(jnp.where(on & (target >= 0) & (target < blocks), 1.0, 0.0))
    m2, m1, p1, p2 = inside
    first, even = place(spacing)
    attended = [
        jnp.where(first, p1, m1),
        jnp.where(even, p2, m2),
        jnp.where(even, m2, p2),
        jnp.where(first, m1, p1),
    ]
    return stack_rows(raw + attended, shape)


def raw_scores(q, keys, flags):
    scores = matmul_nt(jnp.concatenate(keys, axis=0), q) * SCALING
    n = keys[0].shape[0]
    parts = [scores[j * n : (j + 1) * n] for j in range(len(keys))]
    return [s if flag is None else jnp.where(flag > 0.5, s, NEG) for s, flag in zip(parts, flags)]


def top(scores):
    return jnp.max(functools.reduce(jnp.maximum, scores), axis=0, keepdims=True)


def total_of(exps):
    return jnp.sum(functools.reduce(jnp.add, exps), axis=0, keepdims=True)


def near_kernel(
    spacing, blocks, flags_ref, q_ref, g_ref, gain_ref, own, inner, partner,
    exps_ref, lines_ref, grad_ref, on_ref,
):
    rows = q_ref.shape[0]
    heads = q_ref.shape[1] // HEAD_DIM
    on_ref[...] = flag_lines(flags_ref, spacing, blocks, on_ref.shape)
    flags = [None, on_ref[4:5], on_ref[5:6]]
    held = [own, partner, inner]
    peaks, totals = [], []
    for h in range(heads):
        sl = head_slice(h)
        scores = raw_scores(q_ref[:, sl], [r[0, :, sl] for r in held], flags)
        peak = top(scores)
        exps = [jnp.exp(s - peak) for s in scores]
        peaks.append(peak)
        totals.append(total_of(exps))
        for j, e in enumerate(exps):
            at = (h * len(held) + j) * rows
            exps_ref[at : at + rows] = e
        grad_ref[sl] = (g_ref[:, sl].astype(F32) * gain_ref[:, sl]).T
    lines_ref[...] = stack_rows(peaks + totals, lines_ref.shape)


def mid_kernel(q_ref, near_ref, on_ref, outer, exps_ref, lines_ref):
    rows = q_ref.shape[0]
    heads = q_ref.shape[1] // HEAD_DIM
    peaks, totals, factors = [], [], []
    for h in range(heads):
        sl = head_slice(h)
        (score,) = raw_scores(q_ref[:, sl], [outer[0, :, sl]], [on_ref[6:7]])
        before = near_ref[h : h + 1]
        peak = jnp.maximum(before, top([score]))
        exps = jnp.exp(score - peak)
        factor = jnp.exp(before - peak)
        exps_ref[h * rows : (h + 1) * rows] = exps
        peaks.append(peak)
        totals.append(factor * near_ref[heads + h : heads + h + 1] + total_of([exps]))
        factors.append(factor)
    lines_ref[...] = stack_rows(peaks + totals + factors, lines_ref.shape)


def far_kernel(
    q_ref, grad_ref, exps_ref, outer_exps_ref, mid_ref, on_ref, own, partner, inner, outer, fifth,
    attn_ref, stats_ref, sums_ref,
):
    rows = q_ref.shape[0]
    heads = q_ref.shape[1] // HEAD_DIM
    near_rows = exps_ref.shape[0] // heads
    peaks, inverse_totals = [], []
    square = along = 0.0
    for h in range(heads):
        sl = head_slice(h)
        (score,) = raw_scores(q_ref[:, sl], [fifth[0, :, sl]], [on_ref[7:8]])
        before = mid_ref[h : h + 1]
        peak = jnp.maximum(before, top([score]))
        exps = jnp.exp(score - peak)
        factor = jnp.exp(before - peak)
        inverse_total = 1.0 / (factor * mid_ref[heads + h : heads + h + 1] + total_of([exps]))
        outer_factor = factor * inverse_total
        near_factor = mid_ref[2 * heads + h : 2 * heads + h + 1] * outer_factor
        weights = [
            (exps_ref[h * near_rows : (h + 1) * near_rows] * near_factor).astype(BF16),
            (outer_exps_ref[h * rows : (h + 1) * rows] * outer_factor).astype(BF16),
            (exps * inverse_total).astype(BF16),
        ]
        values = [r[1, :, sl] for r in (own, partner, inner, outer, fifth)]
        attn = matmul_tn(jnp.concatenate(values, axis=0), jnp.concatenate(weights, axis=0)).astype(BF16)
        attn_ref[sl] = attn
        wide = attn.astype(F32)
        square = square + wide * wide
        along = along + grad_ref[sl] * wide
        peaks.append(peak)
        inverse_totals.append(inverse_total)
    stats_ref[...] = stack_rows(peaks + inverse_totals, stats_ref.shape)
    sums_ref[...] = stack_rows(
        [jnp.sum(square, axis=0, keepdims=True), jnp.sum(along, axis=0, keepdims=True)],
        sums_ref.shape,
    )


def message_kernel(width, n_parts, *refs):
    on_ref, attn_ref, grad_ref, stats_ref = refs[:4]
    part_refs = refs[4 : 4 + n_parts]
    msg_ref, lines_ref = refs[4 + n_parts :]
    width_here, rows = attn_ref.shape
    heads = width_here // HEAD_DIM
    sums = functools.reduce(jnp.add, [r[...] for r in part_refs])
    inverse = lax.rsqrt(sums[0:1] / width + EPS)
    second = inverse * inverse * inverse * sums[1:2] / width
    line = lambda kind, h: stats_ref[kind * heads + h : kind * heads + h + 1]
    deltas = []
    for h in range(heads):
        sl = head_slice(h)
        attn = attn_ref[sl].astype(F32)
        d_attn = (inverse * grad_ref[sl] - attn * second).astype(BF16)
        msg_ref[sl] = d_attn
        deltas.append(jnp.sum(d_attn.astype(F32) * attn, axis=0, keepdims=True))
    flags = [on_ref[slot : slot + 1] for slot in range(4)]
    for h in range(heads):
        sent = three_parts(line(0, h)) + three_parts(line(1, h)) + three_parts(deltas[h]) + flags
        at = width_here + h * STAT_ROWS
        msg_ref[at : at + STAT_ROWS] = stack_rows(sent, (STAT_ROWS, rows)).astype(BF16)
    lines_ref[...] = stack_rows(deltas + [inverse], lines_ref.shape)


def query_kernel(
    on_ref, q_ref, gain_ref, attn_ref, msg_ref, stats_ref, lines_ref,
    own, partner, inner, outer, fifth, out_ref, dq_ref,
):
    rows = q_ref.shape[0]
    heads = q_ref.shape[1] // HEAD_DIM
    flags = [None] + [on_ref[i : i + 1] for i in range(4, 8)]
    held = [own, partner, inner, outer, fifth]
    inverse = lines_ref[heads : heads + 1]
    for h in range(heads):
        sl = head_slice(h)
        out_ref[:, sl] = ((attn_ref[sl].astype(F32) * inverse).T * gain_ref[:, sl]).astype(BF16)
        keys = [r[0, :, sl] for r in held]
        scores = raw_scores(q_ref[:, sl], keys, flags)
        peak = stats_ref[h : h + 1]
        inverse_total = stats_ref[heads + h : heads + h + 1]
        delta = lines_ref[h : h + 1]
        d_weights = matmul(jnp.concatenate([r[1, :, sl] for r in held], axis=0), msg_ref[sl])
        d_scores = [
            (
                jnp.exp(s - peak)
                * inverse_total
                * (d_weights[j * rows : (j + 1) * rows] - delta)
            ).astype(BF16)
            for j, s in enumerate(scores)
        ]
        dq = matmul_tn(jnp.concatenate(d_scores, axis=0), jnp.concatenate(keys, axis=0))
        dq_ref[:, sl] = (dq * SCALING).astype(BF16)


def key_parts(own, h, q_refs, m_refs, slots, spacing):
    sl = head_slice(h)
    rows, width_here = own.shape[1:]
    first, even = place(spacing)
    queries = jnp.concatenate([r[:, sl] for r in q_refs], axis=0)
    d_attn = jnp.concatenate([r[sl] for r in m_refs], axis=1)
    scores = matmul_nt(own[0, :, sl], queries) * SCALING
    d_weights = matmul(own[1, :, sl], d_attn)
    at = width_here + h * STAT_ROWS
    weights, d_scores = [], []
    for j, (m_ref, slot) in enumerate(zip(m_refs, slots)):
        stats = m_ref[at : at + STAT_ROWS].astype(F32)
        peak = stats[0:1] + stats[1:2] + stats[2:3]
        inverse_total = stats[3:4] + stats[4:5] + stats[5:6]
        delta = stats[6:7] + stats[7:8] + stats[8:9]
        score = scores[:, j * rows : (j + 1) * rows]
        if slot > 0:
            at_m2, at_m1, at_p1, at_p2 = [stats[9 + i : 10 + i] for i in range(4)]
            flag = [
                None,
                jnp.where(first, at_m1, at_p1),
                jnp.where(even, at_m2, at_p2),
                jnp.where(even, at_p2, at_m2),
                jnp.where(first, at_p1, at_m1),
            ][slot]
            score = jnp.where(flag > 0.5, score, NEG)
        weight = jnp.exp(score - peak) * inverse_total
        weights.append(weight.astype(BF16))
        d_scores.append((weight * (d_weights[:, j * rows : (j + 1) * rows] - delta)).astype(BF16))
    d_values = matmul_nt(jnp.concatenate(weights, axis=1), d_attn)
    return matmul(jnp.concatenate(d_scores, axis=1), queries), d_values


def near_key_kernel(spacing, own, q0, q1, q2, q3, m0, m1, m2, m3, dk_ref, dv_ref):
    for h in range(own.shape[2] // HEAD_DIM):
        dk_ref[:, head_slice(h)], dv_ref[:, head_slice(h)] = key_parts(
            own, h, [q0, q1, q2, q3], [m0, m1, m2, m3], (0, 1, 2, 3), spacing
        )


def far_key_kernel(spacing, own, dk_near, dv_near, q4, m4, dk_ref, dv_ref):
    for h in range(own.shape[2] // HEAD_DIM):
        sl = head_slice(h)
        dk, dv = key_parts(own, h, [q4], [m4], (4,), spacing)
        dk_ref[:, sl] = ((dk_near[:, sl] + dk) * SCALING).astype(BF16)
        dv_ref[:, sl] = (dv_near[:, sl] + dv).astype(BF16)


def call(kernel, name, out_shape, args, smem_first=False, cost=None):
    specs = [pl.BlockSpec(memory_space=pltpu.VMEM) for _ in args]
    if smem_first:
        specs[0] = pl.BlockSpec(memory_space=pltpu.SMEM)
    return pl.pallas_call(
        kernel,
        name=name,
        out_shape=out_shape,
        in_specs=specs,
        out_specs=jax.tree.map(lambda _: pl.BlockSpec(memory_space=pltpu.VMEM), out_shape),
        cost_estimate=cost,
        compiler_params=pltpu.CompilerParams(vmem_limit_bytes=VMEM_BYTES),
    )(*args)


def pairs_of(blocks, spacing):
    partner, inner, outer, relay = [], [], [], []
    for i in range(blocks):
        step = i // spacing
        partner.append((i, i + spacing if step % 2 == 0 else i - spacing))
        to = 2 * spacing if (step // 2) % 2 == 0 else -2 * spacing
        if 0 <= i + to < blocks:
            inner.append((i, i + to))
            if 0 <= i + 2 * to < blocks:
                relay.append((i, i + 2 * to))
        if 0 <= i - to < blocks:
            outer.append((i, i - to))
    return partner, inner, outer, relay


def head_sum_parts(sums, devices):
    parts = [sums]
    order = list(range(1, devices))
    for k in order[1:] + order[:1]:
        if devices & (devices - 1) == 0:
            pairs = [(i, i ^ k) for i in range(devices)]
        else:
            pairs = [(i, (i + k) % devices) for i in range(devices)]
        parts.append(lax.ppermute(sums, "head", pairs))
    return parts


def local(queries, keys, values, d_out, gain, blocks_on):
    rows, width_here = queries.shape
    blocks = lax.axis_size("band")
    head_devices = lax.axis_size("head")
    spacing = blocks // 8
    heads = width_here // HEAD_DIM
    width = width_here * head_devices
    gain = gain[None, :]
    partner_pairs, inner_pairs, outer_pairs, relay_pairs = pairs_of(blocks, spacing)
    first, even = place(spacing)

    def wide(lines, dtype=F32):
        return jax.ShapeDtypeStruct((lines, width_here), dtype)

    def narrow(lines, dtype=F32):
        return jax.ShapeDtypeStruct((lines, rows), dtype)

    def to_partner(array):
        return lax.ppermute(array, "band", partner_pairs)

    def swaps(array):
        return [lax.ppermute(array, "band", pairs) for pairs in (inner_pairs, outer_pairs)]

    def passed_on(inner, outer):
        return to_partner(lax.select(first == even, inner, outer))

    own = jnp.stack([keys, values])
    inner, outer = swaps(own)
    partner = to_partner(own)
    q_partner = to_partner(queries)
    exps, near_lines, grad, on = call(
        functools.partial(near_kernel, spacing, blocks),
        "near_attention",
        (narrow(3 * rows * heads), narrow(8), narrow(width_here), narrow(8)),
        (blocks_on, queries, d_out, gain, own, inner, partner),
        smem_first=True,
    )
    exps, q_partner, queries_late = lax.optimization_barrier((exps, q_partner, queries))
    exps, outer = lax.optimization_barrier((exps, outer))
    fifth = passed_on(inner, outer)
    q_inner = lax.ppermute(queries_late, "band", inner_pairs)
    outer_exps, mid_lines = call(
        mid_kernel,
        "mid_attention",
        (narrow(rows * heads), narrow(STAT_ROWS)),
        (queries, near_lines, on, outer),
    )
    attn, stats, sums = call(
        far_kernel,
        "far_attention",
        (narrow(width_here, BF16), narrow(8), narrow(8)),
        (queries, grad, exps, outer_exps, mid_lines, on, own, partner, inner, outer, fifth),
    )
    attn, q_relayed = lax.optimization_barrier((attn, q_inner))
    q_outer = lax.ppermute(q_relayed, "band", relay_pairs)
    parts = head_sum_parts(sums, head_devices)
    q_inner, parts = lax.optimization_barrier((q_inner, parts))
    msg, lines = call(
        functools.partial(message_kernel, width, head_devices),
        "attention_gradient",
        (narrow(width_here + heads * STAT_ROWS, BF16), narrow(8)),
        (on, attn, grad, stats) + tuple(parts),
        cost=pl.CostEstimate(flops=20_000_000_000, bytes_accessed=0, transcendentals=0),
    )
    m_inner, m_outer = swaps(msg)
    m_partner = to_partner(msg)
    out, d_queries = call(
        query_kernel,
        "query_gradient",
        (wide(rows, BF16),) * 2,
        (on, queries, gain, attn, msg, stats, lines, own, partner, inner, outer, fifth),
    )
    q_fifth = passed_on(q_inner, q_outer)
    m_partner, m_inner, m_outer, q_fifth, d_queries = lax.optimization_barrier(
        (m_partner, m_inner, m_outer, q_fifth, d_queries)
    )
    m_fifth = passed_on(m_inner, m_outer)
    dk_near, dv_near = call(
        functools.partial(near_key_kernel, spacing),
        "near_key_gradient",
        (wide(rows),) * 2,
        (own, queries, q_partner, q_inner, q_outer, msg, m_partner, m_inner, m_outer),
    )
    d_keys, d_values = call(
        functools.partial(far_key_kernel, spacing),
        "far_key_gradient",
        (wide(rows, BF16),) * 2,
        (own, dk_near, dv_near, q_fifth, m_fifth),
    )
    return out, d_queries, d_keys, d_values


def solution(mesh):
    in_specs = (
        P("band", "head"),
        P("band", "head"),
        P("band", "head"),
        P("band", "head"),
        P("head"),
        P("band", None),
    )
    out_specs = (P("band", "head"), P("band", "head"), P("band", "head"), P("band", "head"))
    return jax.shard_map(local, mesh=mesh, in_specs=in_specs, out_specs=out_specs, check_vma=False)
```
